768 devices in a mesh: section: 12 (over z), tensor: 16 (over y, core), dp: 4 (over x).
Axes of the slice: x: 4, y: 8, z: 12, core: 2. Of those that a mesh axis runs over, the one named last changes fastest.
Arguments:
- frame_query: bfloat16 [12, 4, 1280, 16], P('section', 'dp', 'tensor'), may hold values from -108 to 108
- frame_key: bfloat16 [12, 4, 1280, 16], P('section', 'dp', 'tensor'), may hold values from -4.5 to 4.5
- frame_value: bfloat16 [12, 4, 1280, 16], P('section', 'dp', 'tensor'), may hold values from -6 to 6
- frame_segment: int32 [12, 4, 16], P('section', 'dp'), may hold values from 0 to 1, never falling along the last dimension, each value on 1 to 12 neighbouring positions
- past_query: bfloat16 [12, 4, 1280, 16], P('section', 'dp', 'tensor'), may hold values from -108 to 108
- past_key: bfloat16 [12, 4, 1280, 16], P('section', 'dp', 'tensor'), may hold values from -4.5 to 4.5
- past_value: bfloat16 [12, 4, 1280, 16], P('section', 'dp', 'tensor'), may hold values from -6 to 6
- past_segment: int32 [12, 4, 16], P('section', 'dp'), may hold values from 0 to 1, never falling along the last dimension, each value on 1 to 12 neighbouring positions
- visual_slot: int32 [4, 192], P('dp'), may hold values from 0 to 191, as said below
- past_slot: int32 [4, 192], P('dp'), may hold values from 0 to 191, as said below
- visual_proj: bfloat16 [1280, 8192], P('tensor'), may hold values from -0.15625 to 0.15625
- layer_weight: bfloat16 [12, 8192, 8192], P('section', 'tensor'), may hold values from -0.0625 to 0.0625
- layer_input: bfloat16 [12, 8192, 768], P('section', 'tensor', 'dp'), may hold values from -6 to 6
- saved_preact: bfloat16 [12, 8192, 768], P('section', 'tensor', 'dp'), may hold values from -8 to 8
- layer_cotangent: bfloat16 [12, 8192, 768], P('section', 'tensor', 'dp'), may hold values from -6 to 6
Outputs:
- forward_out: bfloat16 [12, 8192, 768], P('section', 'tensor', 'dp')
- backward_out: bfloat16 [12, 8192, 768], P('section', 'tensor', 'dp')
- grad_proj: bfloat16 [1280, 8192], P('tensor')
- grad_frames: float32 [3, 12, 4, 1280, 16], P(None, 'section', 'dp', 'tensor')
The draws below stay inside these ranges and needn't reach their ends.
Inputs may be any that keep to these rules, and one draw needn't show every extreme that they name: `visual_slot`: within one replica the 192 positions are distinct. `past_slot`: within one replica the 192 positions are distinct.
All inputs are finite; a program needn't handle non-finite values.
Results may differ from the reference program's by a relative error of at most 0.02.
Values may be sent and summed in bfloat16 or wider, within the bound.
No kernel may reach another device: no remote copies, remote signals or barrier semaphores. Data moves between devices by JAX's collectives and lax.ppermute only.
A program may use at most 64 MiB of HBM per device.

```python
import math
import jax
import jax.numpy as jnp
import numpy as np
from jax import lax

D = 8192
VW = 1280
HEAD_DIM = 80
TOK = 192
VIS = 16
TOKENS = 768
N_SECTION = 12
N_TENSOR = 16
N_DP = 4


def base_field(key, salt):
    return jnp.clip(jax.random.normal(jax.random.fold_in(key, salt), (N_SECTION, N_DP, VW, VIS), jnp.float32), -4.5, 4.5)


def build_key_field(key, salt):
    base_values = base_field(key, salt)
    return base_values.astype(jnp.bfloat16)


def build_query_field(key, salt, own_salt):
    base_values = base_field(key, salt)
    key = jax.random.fold_in(key, own_salt)
    own_values = jnp.clip(jax.random.normal(key, base_values.shape, jnp.float32), -4.5, 4.5)
    return own_values.astype(jnp.bfloat16)


def draw_frame_key(key, part):
    return build_key_field(key, 101)


def draw_frame_query(key, part):
    return build_query_field(key, 101, 2)


def draw_past_key(key, part):
    return build_key_field(key, 202)


def draw_past_query(key, part):
    return build_query_field(key, 202, 4)


def slot_rows(key):

    def draw_replica(replica_key):
        first_key, second_key = jax.random.split(replica_key)
        interior = 1 + jax.random.permutation(first_key, TOK - 2)[:N_SECTION * VIS - 2]
        positions = jnp.concatenate([jnp.array([0, TOK - 1], jnp.int32), interior.astype(jnp.int32)])
        return positions[jax.random.permutation(second_key, N_SECTION * VIS)]
    return jax.vmap(draw_replica)(jax.random.split(key, N_DP)).astype(jnp.int32)


def draw_visual_slot(key, part):
    key = jax.random.fold_in(key, 31)
    return slot_rows(key)


def draw_past_slot(key, part):
    key = jax.random.fold_in(key, 32)
    return slot_rows(key)


def levels(key, dims, cuts, least, high):
    gain, own = 1.0, jax.random.fold_in(key, 6)
    for position, parts in cuts:
        heights = jnp.exp(jax.random.uniform(jax.random.fold_in(own, position), (parts,), jnp.float32, least / len(cuts), high / len(cuts)))
        gain = gain * jnp.repeat(heights, dims[position] // parts).reshape([-1 if axis == position else 1 for axis in range(len(dims))])
    return gain


def profile(number_of, total, reach, skew):
    loads = [(1 << 20) // math.isqrt(standing ** skew) + 1 for standing in range(2, number_of + 1)]
    spare, counts = total - reach - (number_of - 1), [1] * (number_of - 1)
    while spare > 0:
        candidates = [i for i in range(number_of - 1) if counts[i] < reach]
        mass, left = sum([loads[i] for i in candidates]), spare
        for i in candidates:
            extra = min(reach - counts[i], max(1, left * loads[i] // mass), spare)
            counts[i] = counts[i] + extra
            spare = spare - extra
    return np.array([reach] + counts)


def uneven(rng, count, total, most, skew):
    if count == 2:
        one = jax.random.randint(rng, (), max(1, total - most), min(most, total - 1) + 1)
        return jnp.stack([one, total - one])
    tallies = jnp.asarray(profile(count, total, most, skew), jnp.int32)
    pairs = (count - 1) // 2
    source_of, sink = tallies[1:1 + 2 * pairs:2], tallies[2:2 + 2 * pairs:2]
    margin = jnp.minimum(source_of - 1, most - sink)
    passed = jax.random.randint(jax.random.fold_in(rng, 1), (pairs,), 0, 1 << 20) % (margin + 1)
    tallies = tallies.at[1:1 + 2 * pairs:2].set(source_of - passed).at[2:2 + 2 * pairs:2].set(sink + passed)
    return tallies[jax.random.permutation(jax.random.fold_in(rng, 2), count)]


def bell_draw(key, dims, deviation, reach, cuts=(), kind=jnp.bfloat16):
    level = levels(key, dims, cuts, -0.22, 0.18) if cuts else 1.0
    values = jax.random.normal(key, dims, jnp.float32) * deviation * level
    return jnp.minimum(jnp.maximum(values, -reach), reach).astype(kind)


def setup_inputs(seed: int = 0) -> dict:
    key_of = jax.random.split(jax.random.key(seed), 16)
    return {
        "frame_query": draw_frame_query(jax.random.fold_in(key_of[15], 71), 0),
        "frame_key": draw_frame_key(jax.random.fold_in(key_of[15], 71), 0),
        "frame_value": bell_draw(key_of[2], (N_SECTION, N_DP, VW, VIS), 1.0, 6.0, ((0, 12), (1, 4), (2, 16))),
        "frame_segment": jax.vmap(lambda own: jnp.searchsorted(jnp.cumsum(uneven(own, 2, VIS, VIS - VIS // 4, 0)), jnp.arange(VIS), side="right"))(jax.random.split(key_of[3], N_SECTION * N_DP)).reshape((N_SECTION, N_DP, VIS)).astype(jnp.int32),
        "past_query": draw_past_query(jax.random.fold_in(key_of[15], 71), 0),
        "past_key": draw_past_key(jax.random.fold_in(key_of[15], 71), 0),
        "past_value": bell_draw(key_of[6], (N_SECTION, N_DP, VW, VIS), 1.0, 6.0, ((0, 12), (1, 4), (2, 16))),
        "past_segment": jax.vmap(lambda own: jnp.searchsorted(jnp.cumsum(uneven(own, 2, VIS, VIS - VIS // 4, 0)), jnp.arange(VIS), side="right"))(jax.random.split(key_of[7], N_SECTION * N_DP)).reshape((N_SECTION, N_DP, VIS)).astype(jnp.int32),
        "visual_slot": draw_visual_slot(jax.random.fold_in(key_of[15], 71), 0),
        "past_slot": draw_past_slot(jax.random.fold_in(key_of[15], 71), 0),
        "visual_proj": bell_draw(key_of[10], (VW, D), VW ** -0.5, 0.15625, ((0, 16),)),
        "layer_weight": bell_draw(key_of[11], (N_SECTION, D, D), D ** -0.5, 0.0625, ((0, 12), (1, 16))),
        "layer_input": bell_draw(key_of[12], (N_SECTION, D, TOKENS), 1.0, 6.0, ((0, 12), (1, 16), (2, 4))),
        "saved_preact": bell_draw(key_of[13], (N_SECTION, D, TOKENS), 2.0, 8.0, ((0, 12), (1, 16), (2, 4))),
        "layer_cotangent": bell_draw(key_of[14], (N_SECTION, D, TOKENS), 1.0, 6.0, ((0, 12), (1, 16), (2, 4))),
    }


SCORE_FLOOR = -1e+30

def rounded(values):
    return lax.optimization_barrier(values.astype(jnp.bfloat16)).astype(jnp.float32)

def attend(query_rows, key_rows, value_rows, segment):
    head_count = query_rows.shape[0] // HEAD_DIM
    row_total = query_rows.shape[1]
    query_heads = query_rows.reshape(head_count, HEAD_DIM, row_total)
    key_heads = key_rows.reshape(head_count, HEAD_DIM, row_total)
    value_heads = value_rows.reshape(head_count, HEAD_DIM, row_total)
    scores = jnp.einsum('hci,hcj->hij', query_heads, key_heads, precision=lax.Precision.HIGHEST) * HEAD_DIM ** (-0.5)
    same_sample = segment[:, None] == segment[None, :]
    scores = jnp.where(same_sample[None], scores, SCORE_FLOOR)
    row_peak = lax.optimization_barrier(jnp.max(scores, axis=2, keepdims=True))
    exponent = jnp.exp(scores - row_peak)
    probability = rounded(exponent / lax.optimization_barrier(jnp.sum(exponent, axis=2, keepdims=True)))
    mixed = jnp.einsum('hij,hcj->hci', probability, value_heads, precision=lax.Precision.HIGHEST)
    return mixed.reshape(head_count * HEAD_DIM, row_total)

def silu_slope(preact):
    sigmoid_value = jax.nn.sigmoid(preact)
    return sigmoid_value * (1.0 + preact * (1.0 - sigmoid_value))

def reference(frame_query, frame_key, frame_value, frame_segment, past_query, past_key, past_value, past_segment, visual_slot, past_slot, visual_proj, layer_weight, layer_input, saved_preact, layer_cotangent):
    head_rows = VW // N_TENSOR
    model_rows = D // N_TENSOR
    visual_count = N_SECTION * VIS
    group_attend = jax.vmap(jax.vmap(attend))
    current = group_attend(frame_query.astype(jnp.float32), frame_key.astype(jnp.float32), frame_value.astype(jnp.float32), frame_segment).astype(jnp.bfloat16)
    embed_total = jnp.zeros((N_SECTION, N_DP, D, VIS), jnp.float32)
    for block_pos in range(N_TENSOR):
        proj_block = visual_proj[block_pos * head_rows:(block_pos + 1) * head_rows].astype(jnp.float32)
        head_block = current[:, :, block_pos * head_rows:(block_pos + 1) * head_rows].astype(jnp.float32)
        partial_term = jnp.einsum('cd,srci->srdi', proj_block, head_block, precision=lax.Precision.HIGHEST)
        embed_total = embed_total + rounded(partial_term)
    embedded = embed_total.astype(jnp.bfloat16)
    columns = jnp.arange(TOK, dtype=jnp.int32)
    first_parts = []
    for replica in range(N_DP):
        visual_rows = jnp.transpose(embedded[:, replica], (1, 0, 2)).reshape(D, visual_count)
        onehot = (visual_slot[replica][:, None] == columns[None, :]).astype(jnp.bfloat16)
        placed = jnp.dot(visual_rows, onehot, preferred_element_type=jnp.float32).astype(jnp.bfloat16)
        covered = lax.optimization_barrier(jnp.sum(onehot.astype(jnp.float32), axis=0))
        text_rows = layer_input[0, :, replica * TOK:(replica + 1) * TOK]
        first_parts.append(jnp.where(covered[None, :] > 0.5, placed, text_rows))
    first_input = jnp.concatenate(first_parts, axis=1)
    section_input = layer_input.at[0].set(first_input)
    hidden_list = []
    grad_list = []
    for section_pos in range(N_SECTION):
        inputs = section_input[section_pos]
        weight = layer_weight[section_pos]
        preact = jnp.zeros((D, N_DP * TOK), jnp.float32)
        for block_pos in range(N_TENSOR):
            low = block_pos * model_rows
            partial_term = lax.dot_general(weight[low:low + model_rows], inputs[low:low + model_rows], (((0,), (0,)), ((), ())), preferred_element_type=jnp.float32)
            preact = preact + rounded(partial_term)
        hidden_list.append((inputs.astype(jnp.float32) + jax.nn.silu(preact)).astype(jnp.bfloat16))
        upstream = layer_cotangent[section_pos].astype(jnp.float32)
        pre_grad = (upstream * silu_slope(saved_preact[section_pos].astype(jnp.float32))).astype(jnp.bfloat16)
        grad_list.append((upstream + jnp.dot(weight, pre_grad, preferred_element_type=jnp.float32)).astype(jnp.bfloat16))
    zero_block = jnp.zeros((1, D, N_DP * TOK), jnp.bfloat16)
    forward_out = jnp.concatenate([zero_block, jnp.stack(hidden_list[:-1])], axis=0)
    backward_out = jnp.concatenate([jnp.stack(grad_list[1:]), zero_block], axis=0)
    first_grad = grad_list[0]
    grad_parts = []
    for replica in range(N_DP):
        onehot = (past_slot[replica][:, None] == columns[None, :]).astype(jnp.bfloat16)
        picked = lax.dot_general(first_grad[:, replica * TOK:(replica + 1) * TOK], onehot, (((1,), (1,)), ((), ())), preferred_element_type=jnp.float32).astype(jnp.bfloat16)
        grad_parts.append(jnp.transpose(picked.reshape(D, N_SECTION, VIS), (1, 0, 2)))
    visual_grad = jnp.stack(grad_parts, axis=1)

    def past_heads_of(query_all, key_all, value_all):
        return group_attend(query_all, key_all, value_all, past_segment)
    past_float, pullback = jax.vjp(past_heads_of, past_query.astype(jnp.float32), past_key.astype(jnp.float32), past_value.astype(jnp.float32))
    past_heads = past_float.astype(jnp.bfloat16)
    head_grad = jnp.einsum('cd,srdi->srci', visual_proj.astype(jnp.float32), visual_grad.astype(jnp.float32), precision=lax.Precision.HIGHEST).astype(jnp.bfloat16)
    grad_proj = jnp.einsum('srci,srdi->cd', past_heads.astype(jnp.float32), visual_grad.astype(jnp.float32), precision=lax.Precision.HIGHEST).astype(jnp.bfloat16)
    frame_grads = pullback(head_grad.astype(jnp.float32))
    grad_frames = jnp.stack(frame_grads)
    return (forward_out, backward_out, grad_proj, grad_frames)
```

```python
import functools

import jax
import jax.numpy as jnp
from jax import lax
from jax.experimental import pallas as pl
from jax.experimental.pallas import tpu as pltpu
from jax.sharding import PartitionSpec as P

HEAD_DIM = 80


SCORE_FLOOR = -1e30


def attend_parts(query_rows, key_rows, value_rows, segment):
    scores = lax.dot_general(
        query_rows, key_rows, (((0,), (0,)), ((), ())), preferred_element_type=jnp.float32
    ) * HEAD_DIM ** (-0.5)
    same_sample = segment[:, None] == segment[None, :]
    scores = jnp.where(same_sample, scores, SCORE_FLOOR)
    row_peak = jnp.max(scores, axis=1, keepdims=True)
    exponent = jnp.exp(scores - row_peak)
    share = exponent / jnp.sum(exponent, axis=1, keepdims=True)
    weights = share.astype(jnp.bfloat16)
    mixed = lax.dot_general(
        weights, value_rows, (((1,), (1,)), ((), ())), preferred_element_type=jnp.float32
    )
    return mixed.astype(jnp.bfloat16), (query_rows, key_rows, value_rows, share, weights)


def attend_grad(saved, out_grad):
    query_rows, key_rows, value_rows, share, weights = saved
    weight_grad = jnp.dot(out_grad, value_rows, preferred_element_type=jnp.float32)
    score_grad = (
        share
        * (weight_grad - jnp.sum(weight_grad * share, axis=1, keepdims=True))
        * HEAD_DIM ** (-0.5)
    )
    query_grad = lax.dot_general(
        key_rows.astype(jnp.float32),
        score_grad,
        (((1,), (1,)), ((), ())),
        precision=lax.Precision.HIGHEST,
    )
    key_grad = jnp.dot(
        query_rows.astype(jnp.float32), score_grad, precision=lax.Precision.HIGHEST
    )
    value_grad = lax.dot_general(
        out_grad, weights, (((0,), (0,)), ((), ())), preferred_element_type=jnp.float32
    )
    return jnp.stack([query_grad, key_grad, value_grad])


def silu_slope(preact):
    sigmoid_value = jax.nn.sigmoid(preact)
    return sigmoid_value * (1.0 + preact * (1.0 - sigmoid_value))


def shift(value, axis, steps):
    count = lax.axis_size(axis)
    first, last = (max(0, -steps), min(count, count - steps))
    return lax.ppermute(value, axis, [(source, source + steps) for source in range(first, last)])


def rotate(value, axis, steps):
    count = lax.axis_size(axis)
    return lax.ppermute(value, axis, [(i, (i + steps) % count) for i in range(count)])


BLOCK = 4


def to_relays(value):
    count = lax.axis_size("section")
    own = lax.axis_index("section")
    base = jnp.where(own == 0, value, jnp.zeros_like(value))
    arrived = [lax.ppermute(value, "section", [(0, relay)]) for relay in range(BLOCK, count, BLOCK)]
    for piece in arrived:
        base = base + piece
    return base


def block_place(position, relay, count):
    return (relay + position - 1) % count


def spread_columns(base):
    sections, tensors, replicas = (lax.axis_size(axis) for axis in ("section", "tensor", "dp"))
    own = lax.axis_index("dp")
    width = base.shape[1] // replicas
    per_block = tensors // BLOCK

    def device(section, tensor, replica):
        return (section * tensors + tensor) * replicas + replica

    total = None
    for step in range(replicas):
        pairs = [
            (
                device(relay, per_block * position + j, replica),
                device(
                    block_place(position, relay, sections),
                    replicas * j + step,
                    (replica + step) % replicas,
                ),
            )
            for relay in range(0, sections, BLOCK)
            for position in range(BLOCK)
            for j in range(per_block)
            for replica in range(replicas)
        ]
        part = lax.dynamic_slice_in_dim(
            base, lax.rem(own + step, replicas) * width, width, axis=1
        )
        piece = lax.ppermute(part, ("section", "tensor", "dp"), pairs)
        total = piece if total is None else total + piece
    return total


def own_tokens(base, group_rows):
    count = lax.axis_size("section")
    own = lax.axis_index("section")

    def rows_of(section):
        return lax.dynamic_slice_in_dim(base, section * group_rows, group_rows, axis=0)

    total = jnp.where(own % BLOCK == 0, rows_of(own), 0)
    for position in range(BLOCK):
        if position != 1:
            pairs = [
                (relay, block_place(position, relay, count)) for relay in range(0, count, BLOCK)
            ]
            target = lax.rem(own + position - 1 + count, count)
            total = total + lax.ppermute(rows_of(target), "section", pairs)
    return total


def place_kernel(replicas, per_block, own_ref, *refs):
    pieces, out_ref = refs[:-1], refs[-1]
    position, replica = own_ref[0], own_ref[1]
    width = pieces[0].shape[3]
    for step in range(replicas):
        source = lax.rem(replica - step + replicas, replicas)
        for back in range(BLOCK):
            place = lax.rem(position - back + BLOCK, BLOCK)
            for j in range(per_block):
                column = ((place * per_block + j) * replicas + source) * width
                out_ref[:, pl.ds(pl.multiple_of(column, width), width)] = pieces[step][back, j]


def place_columns(own, pieces):
    replicas = len(pieces)
    block, per_block, rows, width = pieces[0].shape
    return pl.pallas_call(
        functools.partial(place_kernel, replicas, per_block),
        out_shape=jax.ShapeDtypeStruct((rows, replicas * block * per_block * width), jnp.bfloat16),
        in_specs=[pl.BlockSpec(memory_space=pltpu.SMEM)]
        + [pl.BlockSpec(memory_space=pltpu.VMEM)] * replicas,
        out_specs=pl.BlockSpec(memory_space=pltpu.VMEM),
        compiler_params=pltpu.CompilerParams(vmem_limit_bytes=16 * 1024 * 1024),
    )(own, *pieces)


def local(
    frame_query,
    frame_key,
    frame_value,
    frame_segment,
    past_query,
    past_key,
    past_value,
    past_segment,
    visual_slot,
    past_slot,
    visual_proj,
    layer_weight,
    layer_input,
    saved_preact,
    layer_cotangent,
):
    section_count = lax.axis_size("section")
    tensor_count = lax.axis_size("tensor")
    replica_count = lax.axis_size("dp")
    own_section = lax.axis_index("section")
    first_flag = own_section == 0
    model_rows = layer_weight.shape[1]
    head_rows = visual_proj.shape[0]
    group_rows = frame_query.shape[3]
    token_count = layer_input.shape[2]
    visual_count = section_count * group_rows
    weight = layer_weight[0]

    upstream = layer_cotangent[0].T.astype(jnp.float32)
    pre_grad = (upstream * silu_slope(saved_preact[0].T.astype(jnp.float32))).astype(jnp.bfloat16)
    pre_full = lax.all_gather(pre_grad, "tensor", axis=1, tiled=True)

    current, _ = attend_parts(
        frame_query[0, 0], frame_key[0, 0], frame_value[0, 0], frame_segment[0, 0]
    )
    past_heads, past_saved = attend_parts(
        past_query[0, 0], past_key[0, 0], past_value[0, 0], past_segment[0, 0]
    )
    columns = jnp.arange(token_count, dtype=jnp.int32)
    slot_table = (visual_slot[0][:, None] == columns[None, :]).astype(jnp.bfloat16)
    past_table = (past_slot[0][:, None] == columns[None, :]).astype(jnp.bfloat16)

    past_all = [past_heads] + [rotate(past_heads, "dp", step) for step in range(1, replica_count)]

    terms = jnp.dot(current, visual_proj, preferred_element_type=jnp.float32).astype(jnp.bfloat16)
    terms = lax.all_to_all(
        terms.reshape(group_rows, tensor_count, model_rows), "tensor", 1, 1, tiled=True
    )
    embedded = jnp.sum(terms.astype(jnp.float32), axis=1).astype(jnp.bfloat16)
    spare = jnp.zeros((group_rows, -(head_rows * replica_count) % 128), jnp.bfloat16)
    parcel = lax.all_gather(
        jnp.concatenate([embedded, *past_all, spare], axis=1), "section", axis=0, tiled=True
    )
    visual_rows = parcel[:, :model_rows]
    past_rows = jnp.concatenate(
        [
            parcel[:, model_rows + step * head_rows : model_rows + (step + 1) * head_rows]
            for step in range(replica_count)
        ],
        axis=0,
    )
    placed = lax.dot_general(
        slot_table, visual_rows, (((0,), (0,)), ((), ())), preferred_element_type=jnp.float32
    ).astype(jnp.bfloat16)
    covered = jnp.sum(slot_table, axis=0, dtype=jnp.float32)
    inputs = jnp.where(first_flag & (covered[:, None] > 0.5), placed, layer_input[0].T)

    input_grad = (
        upstream
        + lax.dot_general(
            pre_full, weight, (((1,), (1,)), ((), ())), preferred_element_type=jnp.float32
        )
    ).astype(jnp.bfloat16)
    visual_grad = jnp.dot(past_table, input_grad, preferred_element_type=jnp.float32).astype(
        jnp.bfloat16
    )

    inputs, visual_grad = lax.optimization_barrier((inputs, visual_grad))
    products = jnp.dot(inputs, weight, preferred_element_type=jnp.float32).astype(jnp.bfloat16)
    preact = lax.psum_scatter(products, "tensor", scatter_dimension=1, tiled=True).astype(
        jnp.float32
    )
    hidden = (inputs.astype(jnp.float32) + jax.nn.silu(preact)).astype(jnp.bfloat16)
    forward_out = shift(hidden, "section", 1)

    backward_out = shift(input_grad, "section", -1)
    base = to_relays(visual_grad)
    piece = spread_columns(base)
    own_grad = own_tokens(base, group_rows)
    gathered = lax.all_gather(piece, "tensor", axis=0)
    per_block = tensor_count // BLOCK
    gathered = gathered.reshape(per_block, replica_count * visual_count, model_rows // replica_count)
    own_columns = jnp.stack(
        [
            lax.dot_general(
                past_rows, gathered[j], (((0,), (0,)), ((), ())), preferred_element_type=jnp.float32
            ).astype(jnp.bfloat16)
            for j in range(per_block)
        ]
    )
    in_block = jnp.stack(
        [own_columns]
        + [
            rotate(own_columns, "section", step if step <= BLOCK // 2 else step - BLOCK)
            for step in range(1, BLOCK)
        ]
    )
    in_block, own_grad = lax.optimization_barrier((in_block, own_grad))
    pieces = [in_block] + [rotate(in_block, "dp", step) for step in range(1, replica_count)]
    position = jnp.stack([lax.rem(own_section + 1, BLOCK), lax.axis_index("dp")]).astype(jnp.int32)
    grad_proj = place_columns(position, pieces)

    own_full = lax.all_gather(own_grad, "tensor", axis=1, tiled=True)
    head_grad = lax.dot_general(
        own_full, visual_proj, (((1,), (1,)), ((), ())), preferred_element_type=jnp.float32
    ).astype(jnp.bfloat16)
    frame_grads = attend_grad(past_saved, head_grad)
    return (forward_out.T[None], backward_out.T[None], grad_proj, frame_grads[:, None, None])


def solution(mesh):
    in_specs = (
        P("section", "dp", "tensor", None),
        P("section", "dp", "tensor", None),
        P("section", "dp", "tensor", None),
        P("section", "dp", None),
        P("section", "dp", "tensor", None),
        P("section", "dp", "tensor", None),
        P("section", "dp", "tensor", None),
        P("section", "dp", None),
        P("dp", None),
        P("dp", None),
        P("tensor", None),
        P("section", "tensor", None),
        P("section", "tensor", "dp"),
        P("section", "tensor", "dp"),
        P("section", "tensor", "dp"),
    )
    out_specs = (
        P("section", "tensor", "dp"),
        P("section", "tensor", "dp"),
        P("tensor", None),
        P(None, "section", "dp", "tensor", None),
    )
    return jax.shard_map(local, mesh=mesh, in_specs=in_specs, out_specs=out_specs, check_vma=False)
```

```python
import functools

import jax
import jax.numpy as jnp
from jax import lax
from jax.experimental import pallas as pl
from jax.experimental.pallas import tpu as pltpu
from jax.sharding import PartitionSpec as P

HEAD_DIM = 80


SCORE_FLOOR = -1e30


def attend_parts(query_rows, key_rows, value_rows, segment):
    scores = lax.dot_general(
        query_rows, key_rows, (((0,), (0,)), ((), ())), preferred_element_type=jnp.float32
    ) * HEAD_DIM ** (-0.5)
    same_sample = segment[:, None] == segment[None, :]
    scores = jnp.where(same_sample, scores, SCORE_FLOOR)
    row_peak = jnp.max(scores, axis=1, keepdims=True)
    exponent = jnp.exp(scores - row_peak)
    share = exponent / jnp.sum(exponent, axis=1, keepdims=True)
    weights = share.astype(jnp.bfloat16)
    mixed = lax.dot_general(
        weights, value_rows, (((1,), (1,)), ((), ())), preferred_element_type=jnp.float32
    )
    return mixed.astype(jnp.bfloat16), (query_rows, key_rows, value_rows, share, weights)


def attend_grad(saved, out_grad):
    query_rows, key_rows, value_rows, share, weights = saved
    weight_grad = jnp.dot(out_grad, value_rows, preferred_element_type=jnp.float32)
    score_grad = (
        share
        * (weight_grad - jnp.sum(weight_grad * share, axis=1, keepdims=True))
        * HEAD_DIM ** (-0.5)
    )
    query_grad = lax.dot_general(
        key_rows.astype(jnp.float32),
        score_grad,
        (((1,), (1,)), ((), ())),
        precision=lax.Precision.HIGHEST,
    )
    key_grad = jnp.dot(
        query_rows.astype(jnp.float32), score_grad, precision=lax.Precision.HIGHEST
    )
    value_grad = lax.dot_general(
        out_grad, weights, (((0,), (0,)), ((), ())), preferred_element_type=jnp.float32
    )
    return jnp.stack([query_grad, key_grad, value_grad])


def silu_slope(preact):
    sigmoid_value = jax.nn.sigmoid(preact)
    return sigmoid_value * (1.0 + preact * (1.0 - sigmoid_value))


def shift(value, axis, steps):
    count = lax.axis_size(axis)
    first, last = (max(0, -steps), min(count, count - steps))
    return lax.ppermute(value, axis, [(source, source + steps) for source in range(first, last)])


def rotate(value, axis, steps):
    count = lax.axis_size(axis)
    return lax.ppermute(value, axis, [(i, (i + steps) % count) for i in range(count)])


BLOCK = 4


def to_relays(value):
    count = lax.axis_size("section")
    own = lax.axis_index("section")
    base = jnp.where(own == 0, value, jnp.zeros_like(value))
    arrived = [lax.ppermute(value, "section", [(0, relay)]) for relay in range(BLOCK, count, BLOCK)]
    for piece in arrived:
        base = base + piece
    return base


def block_place(position, relay, count):
    return (relay + position - 1) % count


def spread_columns(base):
    sections, tensors, replicas = (lax.axis_size(axis) for axis in ("section", "tensor", "dp"))
    own = lax.axis_index("dp")
    width = base.shape[1] // replicas
    per_block = tensors // BLOCK

    def device(section, tensor, replica):
        return (section * tensors + tensor) * replicas + replica

    total = None
    for step in range(replicas):
        pairs = [
            (
                device(relay, per_block * position + j, replica),
                device(
                    block_place(position, relay, sections),
                    replicas * j + step,
                    (replica + step) % replicas,
                ),
            )
            for relay in range(0, sections, BLOCK)
            for position in range(BLOCK)
            for j in range(per_block)
            for replica in range(replicas)
        ]
        part = lax.dynamic_slice_in_dim(
            base, lax.rem(own + step, replicas) * width, width, axis=1
        )
        piece = lax.ppermute(part, ("section", "tensor", "dp"), pairs)
        total = piece if total is None else total + piece
    return total


def place_kernel(shape, own_ref, *refs):
    per_block, rows, width = shape
    pieces, out_ref = refs[:-1], refs[-1]
    position, replica = own_ref[0], own_ref[1]
    replicas = len(pieces)
    for step in range(replicas):
        source = lax.rem(replica - step + replicas, replicas)
        for back in range(BLOCK):
            place = lax.rem(position - back + BLOCK, BLOCK)
            for j in range(per_block):
                first = (back * per_block + j) * rows
                column = ((place * per_block + j) * replicas + source) * width
                out_ref[:, pl.ds(pl.multiple_of(column, width), width)] = pieces[step][
                    first : first + rows, :
                ]


def place_columns(own, pieces, shape):
    replicas = len(pieces)
    per_block, rows, width = shape
    return pl.pallas_call(
        functools.partial(place_kernel, shape),
        out_shape=jax.ShapeDtypeStruct((rows, replicas * BLOCK * per_block * width), jnp.bfloat16),
        in_specs=[pl.BlockSpec(memory_space=pltpu.SMEM)]
        + [pl.BlockSpec(memory_space=pltpu.VMEM)] * replicas,
        out_specs=pl.BlockSpec(memory_space=pltpu.VMEM),
        compiler_params=pltpu.CompilerParams(vmem_limit_bytes=16 * 1024 * 1024),
    )(own, *pieces)


def section_kernel(cotangent_ref, inputs_ref, weight_ref, upstream_ref, product_ref, grad_ref, total):
    step = pl.program_id(0)

    @pl.when(step == 0)
    def _():
        total[...] = upstream_ref[...].astype(jnp.float32)

    total[...] += lax.dot_general(
        cotangent_ref[...],
        weight_ref[...],
        (((1,), (1,)), ((), ())),
        preferred_element_type=jnp.float32,
    )
    product_ref[...] = jnp.dot(
        inputs_ref[...], weight_ref[...], preferred_element_type=jnp.float32
    ).astype(jnp.bfloat16)

    @pl.when(step == pl.num_programs(0) - 1)
    def _():
        grad_ref[...] = total[...].astype(jnp.bfloat16)


def section_products(cotangent, inputs, weight, upstream):
    tokens, rows = inputs.shape
    width = weight.shape[1]
    tile = 2048
    whole = pl.BlockSpec((tokens, rows), lambda n: (0, 0))
    return pl.pallas_call(
        section_kernel,
        grid=(width // tile,),
        in_specs=[
            pl.BlockSpec((tokens, tile), lambda n: (0, n)),
            whole,
            pl.BlockSpec((rows, tile), lambda n: (0, n)),
            whole,
        ],
        out_specs=[pl.BlockSpec((tokens, tile), lambda n: (0, n)), whole],
        out_shape=[
            jax.ShapeDtypeStruct((tokens, width), jnp.bfloat16),
            jax.ShapeDtypeStruct((tokens, rows), jnp.bfloat16),
        ],
        scratch_shapes=[pltpu.VMEM((tokens, rows), jnp.float32)],
        compiler_params=pltpu.CompilerParams(vmem_limit_bytes=56 * 1024 * 1024),
        cost_estimate=pl.CostEstimate(
            flops=4 * tokens * rows * width,
            bytes_accessed=2 * (rows * width + 2 * tokens * width),
            transcendentals=0,
        ),
    )(cotangent, inputs, weight, upstream)


def local(
    frame_query,
    frame_key,
    frame_value,
    frame_segment,
    past_query,
    past_key,
    past_value,
    past_segment,
    visual_slot,
    past_slot,
    visual_proj,
    layer_weight,
    layer_input,
    saved_preact,
    layer_cotangent,
):
    section_count = lax.axis_size("section")
    tensor_count = lax.axis_size("tensor")
    replica_count = lax.axis_size("dp")
    own_section = lax.axis_index("section")
    first_flag = own_section == 0
    model_rows = layer_weight.shape[1]
    head_rows = visual_proj.shape[0]
    group_rows = frame_query.shape[3]
    token_count = layer_input.shape[2]
    visual_count = section_count * group_rows
    weight = layer_weight[0]

    upstream = layer_cotangent[0].T.astype(jnp.float32)
    pre_grad = (upstream * silu_slope(saved_preact[0].T.astype(jnp.float32))).astype(jnp.bfloat16)
    pre_full = lax.all_gather(pre_grad, "tensor", axis=1, tiled=True)

    current, _ = attend_parts(
        frame_query[0, 0], frame_key[0, 0], frame_value[0, 0], frame_segment[0, 0]
    )
    past_heads, past_saved = attend_parts(
        past_query[0, 0], past_key[0, 0], past_value[0, 0], past_segment[0, 0]
    )
    columns = jnp.arange(token_count, dtype=jnp.int32)
    slot_table = (visual_slot[0][:, None] == columns[None, :]).astype(jnp.bfloat16)
    past_table = (past_slot[0][:, None] == columns[None, :]).astype(jnp.bfloat16)

    terms = jnp.dot(current, visual_proj, preferred_element_type=jnp.float32).astype(jnp.bfloat16)
    terms = lax.all_to_all(
        terms.reshape(group_rows, tensor_count, model_rows), "tensor", 1, 1, tiled=True
    )
    embedded = jnp.sum(terms.astype(jnp.float32), axis=1).astype(jnp.bfloat16)
    spare = jnp.zeros((group_rows, -head_rows % 128), jnp.bfloat16)
    parcel = lax.all_gather(
        jnp.concatenate([embedded, past_heads, spare], axis=1), "section", axis=0, tiled=True
    )
    visual_rows = parcel[:, :model_rows]
    past_rows = parcel[:, model_rows : model_rows + head_rows]
    placed = lax.dot_general(
        slot_table, visual_rows, (((0,), (0,)), ((), ())), preferred_element_type=jnp.float32
    ).astype(jnp.bfloat16)
    covered = jnp.sum(slot_table, axis=0, dtype=jnp.float32)
    inputs = jnp.where(first_flag & (covered[:, None] > 0.5), placed, layer_input[0].T)

    products, input_grad = section_products(pre_full, inputs, weight, layer_cotangent[0].T)
    preact = lax.psum_scatter(products, "tensor", scatter_dimension=1, tiled=True).astype(
        jnp.float32
    )
    hidden = (inputs.astype(jnp.float32) + jax.nn.silu(preact)).astype(jnp.bfloat16)
    forward_out = shift(hidden, "section", 1)
    backward_out = shift(input_grad, "section", -1)

    visual_grad = jnp.dot(past_table, input_grad, preferred_element_type=jnp.float32).astype(
        jnp.bfloat16
    )
    base = to_relays(visual_grad)
    gathered = lax.all_gather(spread_columns(base), "tensor", axis=0)
    past_rows = jnp.concatenate(
        [past_rows] + [rotate(past_rows, "dp", step) for step in range(1, replica_count)], axis=0
    )
    per_block = tensor_count // BLOCK
    part_width = model_rows // replica_count
    position, replica = lax.rem(own_section + 1, BLOCK), lax.axis_index("dp")
    gathered = gathered.reshape(per_block, replica_count * visual_count, part_width)
    own_columns, head_part = [], 0.0
    for j in range(per_block):
        own_columns.append(
            lax.dot_general(
                past_rows, gathered[j], (((0,), (0,)), ((), ())), preferred_element_type=jnp.float32
            ).astype(jnp.bfloat16)
        )
        proj_part = lax.dynamic_slice_in_dim(
            visual_proj,
            (position * per_block + j) * model_rows + replica * part_width,
            part_width,
            axis=1,
        )
        proj_part = jnp.pad(proj_part, ((0, part_width - head_rows), (0, 0)))
        head_part = head_part + lax.dot_general(
            gathered[j], proj_part, (((1,), (1,)), ((), ())), preferred_element_type=jnp.float32
        )
    own_columns = jnp.concatenate(own_columns, axis=0)
    head_part = head_part.astype(jnp.bfloat16).reshape(
        replica_count, section_count, group_rows, part_width
    )

    def head_of(section):
        return lax.dynamic_index_in_dim(head_part, section, axis=1, keepdims=False).reshape(
            replica_count * group_rows, part_width
        )

    column_rows = own_columns.shape[0]
    in_block, head_sum = [own_columns], head_of(own_section).astype(jnp.float32)
    for step in range(1, BLOCK):
        hops = step if step <= BLOCK // 2 else step - BLOCK
        target = lax.rem(own_section + hops + section_count, section_count)
        arrived = rotate(
            jnp.concatenate([own_columns, head_of(target)], axis=0), "section", hops
        )
        in_block.append(arrived[:column_rows])
        head_sum = head_sum + arrived[column_rows:].astype(jnp.float32)

    bundle = jnp.concatenate(in_block + [head_sum.astype(jnp.bfloat16)], axis=0)
    pieces, head_grad = [bundle], head_sum[:group_rows]
    for step in range(1, replica_count):
        arrived = rotate(bundle, "dp", step)
        first = BLOCK * column_rows + (replica_count - step) * group_rows
        head_grad = head_grad + arrived[first : first + group_rows].astype(jnp.float32)
        pieces.append(arrived)
    head_grad = head_grad[:, :head_rows].astype(jnp.bfloat16)
    grad_proj = place_columns(
        jnp.stack([position, replica]).astype(jnp.int32), pieces, (per_block, head_rows, part_width)
    )
    frame_grads = attend_grad(past_saved, head_grad)
    return (forward_out.T[None], backward_out.T[None], grad_proj, frame_grads[:, None, None])


def solution(mesh):
    in_specs = (
        P("section", "dp", "tensor", None),
        P("section", "dp", "tensor", None),
        P("section", "dp", "tensor", None),
        P("section", "dp", None),
        P("section", "dp", "tensor", None),
        P("section", "dp", "tensor", None),
        P("section", "dp", "tensor", None),
        P("section", "dp", None),
        P("dp", None),
        P("dp", None),
        P("tensor", None),
        P("section", "tensor", None),
        P("section", "tensor", "dp"),
        P("section", "tensor", "dp"),
        P("section", "tensor", "dp"),
    )
    out_specs = (
        P("section", "tensor", "dp"),
        P("section", "tensor", "dp"),
        P("tensor", None),
        P(None, "section", "dp", "tensor", None),
    )
    return jax.shard_map(local, mesh=mesh, in_specs=in_specs, out_specs=out_specs, check_vma=False)
```

```python
import functools

import jax
import jax.numpy as jnp
from jax import lax
from jax.experimental import pallas as pl
from jax.experimental.pallas import tpu as pltpu
from jax.sharding import PartitionSpec as P

HEAD_DIM = 80


SCORE_FLOOR = -1e30


def attend_parts(query_rows, key_rows, value_rows, segment):
    scores = lax.dot_general(
        query_rows, key_rows, (((0,), (0,)), ((), ())), preferred_element_type=jnp.float32
    ) * HEAD_DIM ** (-0.5)
    same_sample = segment[:, None] == segment[None, :]
    scores = jnp.where(same_sample, scores, SCORE_FLOOR)
    row_peak = jnp.max(scores, axis=1, keepdims=True)
    exponent = jnp.exp(scores - row_peak)
    share = exponent / jnp.sum(exponent, axis=1, keepdims=True)
    weights = share.astype(jnp.bfloat16)
    mixed = lax.dot_general(
        weights, value_rows, (((1,), (1,)), ((), ())), preferred_element_type=jnp.float32
    )
    return mixed.astype(jnp.bfloat16), (query_rows, key_rows, value_rows, share, weights)


def attend_grad(saved, out_grad):
    query_rows, key_rows, value_rows, share, weights = saved
    weight_grad = jnp.dot(out_grad, value_rows, preferred_element_type=jnp.float32)
    score_grad = (
        share
        * (weight_grad - jnp.sum(weight_grad * share, axis=1, keepdims=True))
        * HEAD_DIM ** (-0.5)
    )
    query_grad = lax.dot_general(
        key_rows.astype(jnp.float32),
        score_grad,
        (((1,), (1,)), ((), ())),
        precision=lax.Precision.HIGHEST,
    )
    key_grad = jnp.dot(
        query_rows.astype(jnp.float32), score_grad, precision=lax.Precision.HIGHEST
    )
    value_grad = lax.dot_general(
        out_grad, weights, (((0,), (0,)), ((), ())), preferred_element_type=jnp.float32
    )
    return jnp.stack([query_grad, key_grad, value_grad])


def silu_slope(preact):
    sigmoid_value = jax.nn.sigmoid(preact)
    return sigmoid_value * (1.0 + preact * (1.0 - sigmoid_value))


def shift(value, axis, steps):
    count = lax.axis_size(axis)
    first, last = (max(0, -steps), min(count, count - steps))
    return lax.ppermute(value, axis, [(source, source + steps) for source in range(first, last)])


def rotate(value, axis, steps):
    count = lax.axis_size(axis)
    return lax.ppermute(value, axis, [(i, (i + steps) % count) for i in range(count)])


BLOCK = 4


def to_relays(value):
    count = lax.axis_size("section")
    own = lax.axis_index("section")
    base = jnp.where(own == 0, value, jnp.zeros_like(value))
    arrived = [lax.ppermute(value, "section", [(0, relay)]) for relay in range(BLOCK, count, BLOCK)]
    for piece in arrived:
        base = base + piece
    return base


def block_place(position, relay, count):
    return (relay + position - 1) % count


def spread_columns(base):
    sections, tensors, replicas = (lax.axis_size(axis) for axis in ("section", "tensor", "dp"))
    own = lax.axis_index("dp")
    width = base.shape[1] // replicas
    per_block = tensors // BLOCK

    def device(section, tensor, replica):
        return (section * tensors + tensor) * replicas + replica

    total = None
    for step in range(replicas):
        pairs = [
            (
                device(relay, per_block * position + j, replica),
                device(
                    block_place(position, relay, sections),
                    replicas * j + step,
                    (replica + step) % replicas,
                ),
            )
            for relay in range(0, sections, BLOCK)
            for position in range(BLOCK)
            for j in range(per_block)
            for replica in range(replicas)
        ]
        part = lax.dynamic_slice_in_dim(
            base, lax.rem(own + step, replicas) * width, width, axis=1
        )
        piece = lax.ppermute(part, ("section", "tensor", "dp"), pairs)
        total = piece if total is None else total + piece
    return total


def place_kernel(shape, own_ref, own, before, upper, lower, after, out_ref):
    per_block, rows, width = shape
    position, replica = own_ref[0], own_ref[1]
    cut = upper.shape[0]
    for step in range(4):
        source = lax.rem(replica + 4 - step, 4)
        for back in range(BLOCK):
            place = lax.rem(position - back + BLOCK, BLOCK)
            for j in range(per_block):
                first = (back * per_block + j) * rows
                if step == 2:
                    piece, first = (upper, first) if first < cut else (lower, first - cut)
                else:
                    piece = {0: own, 1: before, 3: after}[step]
                column = ((place * per_block + j) * 4 + source) * width
                out_ref[:, pl.ds(pl.multiple_of(column, width), width)] = piece[
                    first : first + rows, :
                ]


def place_columns(own, pieces, shape):
    per_block, rows, width = shape
    return pl.pallas_call(
        functools.partial(place_kernel, shape),
        out_shape=jax.ShapeDtypeStruct((rows, 4 * BLOCK * per_block * width), jnp.bfloat16),
        in_specs=[pl.BlockSpec(memory_space=pltpu.SMEM)]
        + [pl.BlockSpec(memory_space=pltpu.VMEM)] * len(pieces),
        out_specs=pl.BlockSpec(memory_space=pltpu.VMEM),
        compiler_params=pltpu.CompilerParams(vmem_limit_bytes=16 * 1024 * 1024),
    )(own, *pieces)


def section_kernel(
    cotangent_ref,
    inputs_ref,
    weight_ref,
    upstream_ref,
    table_ref,
    product_ref,
    grad_ref,
    picked_ref,
    total,
):
    step = pl.program_id(0)

    @pl.when(step == 0)
    def _():
        total[...] = upstream_ref[...].astype(jnp.float32)

    total[...] += lax.dot_general(
        cotangent_ref[...],
        weight_ref[...],
        (((1,), (1,)), ((), ())),
        preferred_element_type=jnp.float32,
    )
    product_ref[...] = jnp.dot(
        inputs_ref[...], weight_ref[...], preferred_element_type=jnp.float32
    ).astype(jnp.bfloat16)

    @pl.when(step == pl.num_programs(0) - 1)
    def _():
        grad = total[...].astype(jnp.bfloat16)
        grad_ref[...] = grad
        picked_ref[...] = jnp.dot(
            table_ref[...], grad, preferred_element_type=jnp.float32
        ).astype(jnp.bfloat16)


def section_products(cotangent, inputs, weight, upstream, table):
    tokens, rows = inputs.shape
    width = weight.shape[1]
    tile = 2048
    whole = pl.BlockSpec((tokens, rows), lambda n: (0, 0))
    return pl.pallas_call(
        section_kernel,
        grid=(width // tile,),
        in_specs=[
            pl.BlockSpec((tokens, tile), lambda n: (0, n)),
            whole,
            pl.BlockSpec((rows, tile), lambda n: (0, n)),
            whole,
            pl.BlockSpec(table.shape, lambda n: (0, 0)),
        ],
        out_specs=[
            pl.BlockSpec((tokens, tile), lambda n: (0, n)),
            whole,
            pl.BlockSpec((table.shape[0], rows), lambda n: (0, 0)),
        ],
        out_shape=[
            jax.ShapeDtypeStruct((tokens, width), jnp.bfloat16),
            jax.ShapeDtypeStruct((tokens, rows), jnp.bfloat16),
            jax.ShapeDtypeStruct((table.shape[0], rows), jnp.bfloat16),
        ],
        scratch_shapes=[pltpu.VMEM((tokens, rows), jnp.float32)],
        compiler_params=pltpu.CompilerParams(vmem_limit_bytes=56 * 1024 * 1024),
        cost_estimate=pl.CostEstimate(
            flops=4 * tokens * rows * width,
            bytes_accessed=2 * (rows * width + 2 * tokens * width),
            transcendentals=0,
        ),
    )(cotangent, inputs, weight, upstream, table)


def local(
    frame_query,
    frame_key,
    frame_value,
    frame_segment,
    past_query,
    past_key,
    past_value,
    past_segment,
    visual_slot,
    past_slot,
    visual_proj,
    layer_weight,
    layer_input,
    saved_preact,
    layer_cotangent,
):
    section_count = lax.axis_size("section")
    tensor_count = lax.axis_size("tensor")
    replica_count = lax.axis_size("dp")
    own_section = lax.axis_index("section")
    first_flag = own_section == 0
    model_rows = layer_weight.shape[1]
    head_rows = visual_proj.shape[0]
    group_rows = frame_query.shape[3]
    token_count = layer_input.shape[2]
    visual_count = section_count * group_rows
    weight = layer_weight[0]

    upstream = layer_cotangent[0].T.astype(jnp.float32)
    pre_grad = (upstream * silu_slope(saved_preact[0].T.astype(jnp.float32))).astype(jnp.bfloat16)
    pre_full = lax.all_gather(pre_grad, "tensor", axis=1, tiled=True)

    current, _ = attend_parts(
        frame_query[0, 0], frame_key[0, 0], frame_value[0, 0], frame_segment[0, 0]
    )
    past_heads, past_saved = attend_parts(
        past_query[0, 0], past_key[0, 0], past_value[0, 0], past_segment[0, 0]
    )
    columns = jnp.arange(token_count, dtype=jnp.int32)
    slot_table = (visual_slot[0][:, None] == columns[None, :]).astype(jnp.bfloat16)
    past_table = (past_slot[0][:, None] == columns[None, :]).astype(jnp.bfloat16)

    past_all = [past_heads] + [rotate(past_heads, "dp", step) for step in range(1, replica_count)]

    terms = jnp.dot(current, visual_proj, preferred_element_type=jnp.float32).astype(jnp.bfloat16)
    terms = lax.all_to_all(
        terms.reshape(group_rows, tensor_count, model_rows), "tensor", 1, 1, tiled=True
    )
    embedded = jnp.sum(terms.astype(jnp.float32), axis=1).astype(jnp.bfloat16)
    spare = jnp.zeros((group_rows, -(head_rows * replica_count) % 128), jnp.bfloat16)
    parcel = lax.all_gather(
        jnp.concatenate([embedded, *past_all, spare], axis=1), "section", axis=0, tiled=True
    )
    visual_rows = parcel[:, :model_rows]
    past_rows = jnp.concatenate(
        [
            parcel[:, model_rows + step * head_rows : model_rows + (step + 1) * head_rows]
            for step in range(replica_count)
        ],
        axis=0,
    )
    placed = lax.dot_general(
        slot_table, visual_rows, (((0,), (0,)), ((), ())), preferred_element_type=jnp.float32
    ).astype(jnp.bfloat16)
    covered = jnp.sum(slot_table, axis=0, dtype=jnp.float32)
    inputs = jnp.where(first_flag & (covered[:, None] > 0.5), placed, layer_input[0].T)

    products, input_grad, visual_grad = section_products(
        pre_full, inputs, weight, layer_cotangent[0].T, past_table
    )
    preact = lax.psum_scatter(products, "tensor", scatter_dimension=1, tiled=True).astype(
        jnp.float32
    )
    hidden = (inputs.astype(jnp.float32) + jax.nn.silu(preact)).astype(jnp.bfloat16)
    backward_out = shift(input_grad, "section", -1)

    base = to_relays(visual_grad)
    piece, backward_out = lax.optimization_barrier((spread_columns(base), backward_out))
    gathered = lax.all_gather(piece, "tensor", axis=0)
    per_block = tensor_count // BLOCK
    part_width = model_rows // replica_count
    position, replica = lax.rem(own_section + 1, BLOCK), lax.axis_index("dp")
    gathered = gathered.reshape(per_block, replica_count * visual_count, part_width)
    own_columns, head_part = [], 0.0
    for j in range(per_block):
        own_columns.append(
            lax.dot_general(
                past_rows, gathered[j], (((0,), (0,)), ((), ())), preferred_element_type=jnp.float32
            ).astype(jnp.bfloat16)
        )
        proj_part = lax.dynamic_slice_in_dim(
            visual_proj,
            (position * per_block + j) * model_rows + replica * part_width,
            part_width,
            axis=1,
        )
        proj_part = jnp.pad(proj_part, ((0, part_width - head_rows), (0, 0)))
        head_part = head_part + lax.dot_general(
            gathered[j], proj_part, (((1,), (1,)), ((), ())), preferred_element_type=jnp.float32
        )
    own_columns = jnp.concatenate(own_columns, axis=0)
    head_part = head_part.astype(jnp.bfloat16).reshape(
        replica_count, section_count, group_rows, part_width
    )

    def head_of(section):
        return lax.dynamic_index_in_dim(head_part, section, axis=1, keepdims=False).reshape(
            replica_count * group_rows, part_width
        )

    column_rows = own_columns.shape[0]
    in_block, head_sum = [own_columns], head_of(own_section).astype(jnp.float32)
    for step in range(1, BLOCK):
        hops = step if step <= BLOCK // 2 else step - BLOCK
        target = lax.rem(own_section + hops + section_count, section_count)
        arrived = rotate(
            jnp.concatenate([own_columns, head_of(target)], axis=0), "section", hops
        )
        in_block.append(arrived[:column_rows])
        head_sum = head_sum + arrived[column_rows:].astype(jnp.float32)

    bundle = jnp.concatenate(in_block + [head_sum.astype(jnp.bfloat16)], axis=0)
    before, after, hidden = lax.optimization_barrier(
        (rotate(bundle, "dp", 1), rotate(bundle, "dp", -1), hidden)
    )
    forward_out = shift(hidden, "section", 1)
    cut = BLOCK * column_rows // 2
    upper, lower = rotate(before[:cut], "dp", 1), rotate(after[cut:], "dp", -1)
    halves = [(bundle[:cut], bundle[cut:]), (before[:cut], before[cut:]), (upper, lower)]
    halves.append((after[:cut], after[cut:]))
    head_grad = head_sum[:group_rows]
    for step in range(1, replica_count):
        first = BLOCK * column_rows + (replica_count - step) * group_rows - cut
        head_grad = head_grad + halves[step][1][first : first + group_rows].astype(jnp.float32)
    head_grad = head_grad[:, :head_rows].astype(jnp.bfloat16)
    grad_proj = place_columns(
        jnp.stack([position, replica]).astype(jnp.int32),
        (bundle, before, upper, lower, after),
        (per_block, head_rows, part_width),
    )
    frame_grads = attend_grad(past_saved, head_grad)
    return (forward_out.T[None], backward_out.T[None], grad_proj, frame_grads[:, None, None])


def solution(mesh):
    in_specs = (
        P("section", "dp", "tensor", None),
        P("section", "dp", "tensor", None),
        P("section", "dp", "tensor", None),
        P("section", "dp", None),
        P("section", "dp", "tensor", None),
        P("section", "dp", "tensor", None),
        P("section", "dp", "tensor", None),
        P("section", "dp", None),
        P("dp", None),
        P("dp", None),
        P("tensor", None),
        P("section", "tensor", None),
        P("section", "tensor", "dp"),
        P("section", "tensor", "dp"),
        P("section", "tensor", "dp"),
    )
    out_specs = (
        P("section", "tensor", "dp"),
        P("section", "tensor", "dp"),
        P("tensor", None),
        P(None, "section", "dp", "tensor", None),
    )
    return jax.shard_map(local, mesh=mesh, in_specs=in_specs, out_specs=out_specs, check_vma=False)
```

```python
import functools

import jax
import jax.numpy as jnp
from jax import lax
from jax.experimental import pallas as pl
from jax.experimental.pallas import tpu as pltpu
from jax.sharding import PartitionSpec as P

HEAD_DIM = 80


SCORE_FLOOR = -1e30


def attend_parts(query_rows, key_rows, value_rows, segment):
    scores = lax.dot_general(
        query_rows, key_rows, (((0,), (0,)), ((), ())), preferred_element_type=jnp.float32
    ) * HEAD_DIM ** (-0.5)
    same_sample = segment[:, None] == segment[None, :]
    scores = jnp.where(same_sample, scores, SCORE_FLOOR)
    row_peak = jnp.max(scores, axis=1, keepdims=True)
    exponent = jnp.exp(scores - row_peak)
    share = exponent / jnp.sum(exponent, axis=1, keepdims=True)
    weights = share.astype(jnp.bfloat16)
    mixed = lax.dot_general(
        weights, value_rows, (((1,), (1,)), ((), ())), preferred_element_type=jnp.float32
    )
    return mixed.astype(jnp.bfloat16), (query_rows, key_rows, value_rows, share, weights)


def attend_grad(saved, out_grad):
    query_rows, key_rows, value_rows, share, weights = saved
    weight_grad = jnp.dot(out_grad, value_rows, preferred_element_type=jnp.float32)
    score_grad = (
        share
        * (weight_grad - jnp.sum(weight_grad * share, axis=1, keepdims=True))
        * HEAD_DIM ** (-0.5)
    )
    query_grad = lax.dot_general(
        key_rows.astype(jnp.float32),
        score_grad,
        (((1,), (1,)), ((), ())),
        precision=lax.Precision.HIGHEST,
    )
    key_grad = jnp.dot(
        query_rows.astype(jnp.float32), score_grad, precision=lax.Precision.HIGHEST
    )
    value_grad = lax.dot_general(
        out_grad, weights, (((0,), (0,)), ((), ())), preferred_element_type=jnp.float32
    )
    return jnp.stack([query_grad, key_grad, value_grad])


def silu_slope(preact):
    sigmoid_value = jax.nn.sigmoid(preact)
    return sigmoid_value * (1.0 + preact * (1.0 - sigmoid_value))


def shift(value, axis, steps):
    count = lax.axis_size(axis)
    first, last = (max(0, -steps), min(count, count - steps))
    return lax.ppermute(value, axis, [(source, source + steps) for source in range(first, last)])


def rotate(value, axis, steps):
    count = lax.axis_size(axis)
    return lax.ppermute(value, axis, [(i, (i + steps) % count) for i in range(count)])


BLOCK = 4


def to_relays(value):
    count = lax.axis_size("section")
    own = lax.axis_index("section")
    base = jnp.where(own == 0, value, jnp.zeros_like(value))
    arrived = [lax.ppermute(value, "section", [(0, relay)]) for relay in range(BLOCK, count, BLOCK)]
    for piece in arrived:
        base = base + piece
    return base


def block_place(position, relay, count):
    return (relay + position - 1) % count


def spread_columns(base):
    sections, tensors, replicas = (lax.axis_size(axis) for axis in ("section", "tensor", "dp"))
    own = lax.axis_index("dp")
    width = base.shape[1] // replicas
    per_block = tensors // BLOCK

    def device(section, tensor, replica):
        return (section * tensors + tensor) * replicas + replica

    total = None
    for step in range(replicas):
        pairs = [
            (
                device(relay, per_block * position + j, replica),
                device(
                    block_place(position, relay, sections),
                    replicas * j + step,
                    (replica + step) % replicas,
                ),
            )
            for relay in range(0, sections, BLOCK)
            for position in range(BLOCK)
            for j in range(per_block)
            for replica in range(replicas)
        ]
        part = lax.dynamic_slice_in_dim(
            base, lax.rem(own + step, replicas) * width, width, axis=1
        )
        piece = lax.ppermute(part, ("section", "tensor", "dp"), pairs)
        total = piece if total is None else total + piece
    return total


def place_kernel(shape, own_ref, *refs):
    per_block, rows, width = shape
    pieces, out_ref = refs[:-1], refs[-1]
    position, replica = own_ref[0], own_ref[1]
    replicas = len(pieces)
    for step in range(replicas):
        source = lax.rem(replica - step + replicas, replicas)
        for back in range(BLOCK):
            place = lax.rem(position - back + BLOCK, BLOCK)
            for j in range(per_block):
                first = (back * per_block + j) * rows
                column = ((place * per_block + j) * replicas + source) * width
                out_ref[:, pl.ds(pl.multiple_of(column, width), width)] = pieces[step][
                    first : first + rows, :
                ]


def place_columns(own, pieces, shape):
    per_block, rows, width = shape
    return pl.pallas_call(
        functools.partial(place_kernel, shape),
        out_shape=jax.ShapeDtypeStruct(
            (rows, len(pieces) * BLOCK * per_block * width), jnp.bfloat16
        ),
        in_specs=[pl.BlockSpec(memory_space=pltpu.SMEM)]
        + [pl.BlockSpec(memory_space=pltpu.VMEM)] * len(pieces),
        out_specs=pl.BlockSpec(memory_space=pltpu.VMEM),
        compiler_params=pltpu.CompilerParams(vmem_limit_bytes=16 * 1024 * 1024),
    )(own, *pieces)


def section_kernel(
    cotangent_ref,
    inputs_ref,
    weight_ref,
    upstream_ref,
    slot_ref,
    product_ref,
    grad_ref,
    picked_ref,
    total,
):
    step = pl.program_id(0)

    @pl.when(step == 0)
    def _():
        total[...] = upstream_ref[...].astype(jnp.float32)

    total[...] += lax.dot_general(
        cotangent_ref[...],
        weight_ref[...],
        (((1,), (1,)), ((), ())),
        preferred_element_type=jnp.float32,
    )
    product_ref[...] = jnp.dot(
        inputs_ref[...], weight_ref[...], preferred_element_type=jnp.float32
    ).astype(jnp.bfloat16)

    @pl.when(step == pl.num_programs(0) - 1)
    def _():
        grad = total[...].astype(jnp.bfloat16)
        grad_ref[...] = grad
        tokens, count = grad.shape[0], slot_ref.shape[1]
        table = lax.broadcasted_iota(jnp.int32, (tokens, count), 0) == slot_ref[...]
        picked_ref[...] = lax.dot_general(
            table.astype(jnp.float32).astype(jnp.bfloat16),
            grad,
            (((0,), (0,)), ((), ())),
            preferred_element_type=jnp.float32,
        ).astype(jnp.bfloat16)


def section_products(cotangent, inputs, weight, upstream, slot):
    tokens, rows = inputs.shape
    width = weight.shape[1]
    tile = 2048
    whole = pl.BlockSpec((tokens, rows), lambda n: (0, 0))
    return pl.pallas_call(
        section_kernel,
        grid=(width // tile,),
        in_specs=[
            pl.BlockSpec((tokens, tile), lambda n: (0, n)),
            whole,
            pl.BlockSpec((rows, tile), lambda n: (0, n)),
            whole,
            pl.BlockSpec(slot.shape, lambda n: (0, 0)),
        ],
        out_specs=[
            pl.BlockSpec((tokens, tile), lambda n: (0, n)),
            whole,
            pl.BlockSpec((slot.shape[1], rows), lambda n: (0, 0)),
        ],
        out_shape=[
            jax.ShapeDtypeStruct((tokens, width), jnp.bfloat16),
            jax.ShapeDtypeStruct((tokens, rows), jnp.bfloat16),
            jax.ShapeDtypeStruct((slot.shape[1], rows), jnp.bfloat16),
        ],
        scratch_shapes=[pltpu.VMEM((tokens, rows), jnp.float32)],
        compiler_params=pltpu.CompilerParams(vmem_limit_bytes=56 * 1024 * 1024),
        cost_estimate=pl.CostEstimate(
            flops=4 * tokens * rows * width,
            bytes_accessed=2 * (rows * width + 2 * tokens * width),
            transcendentals=0,
        ),
    )(cotangent, inputs, weight, upstream, slot)


def local(
    frame_query,
    frame_key,
    frame_value,
    frame_segment,
    past_query,
    past_key,
    past_value,
    past_segment,
    visual_slot,
    past_slot,
    visual_proj,
    layer_weight,
    layer_input,
    saved_preact,
    layer_cotangent,
):
    section_count = lax.axis_size("section")
    tensor_count = lax.axis_size("tensor")
    replica_count = lax.axis_size("dp")
    own_section = lax.axis_index("section")
    first_flag = own_section == 0
    model_rows = layer_weight.shape[1]
    head_rows = visual_proj.shape[0]
    group_rows = frame_query.shape[3]
    token_count = layer_input.shape[2]
    visual_count = section_count * group_rows
    weight = layer_weight[0]

    upstream = layer_cotangent[0].T.astype(jnp.float32)
    pre_grad = (upstream * silu_slope(saved_preact[0].T.astype(jnp.float32))).astype(jnp.bfloat16)
    pre_full = lax.all_gather(pre_grad, "tensor", axis=1, tiled=True)

    current, _ = attend_parts(
        frame_query[0, 0], frame_key[0, 0], frame_value[0, 0], frame_segment[0, 0]
    )
    columns = jnp.arange(token_count, dtype=jnp.int32)
    slot_table = (visual_slot[0][:, None] == columns[None, :]).astype(jnp.bfloat16)

    terms = jnp.dot(current, visual_proj, preferred_element_type=jnp.float32).astype(jnp.bfloat16)
    terms = jnp.transpose(terms.reshape(group_rows, tensor_count, model_rows), (1, 0, 2))
    terms, past_query, past_key = lax.optimization_barrier((terms, past_query, past_key))
    past_heads, past_saved = attend_parts(
        past_query[0, 0], past_key[0, 0], past_value[0, 0], past_segment[0, 0]
    )

    past_all = [past_heads] + [rotate(past_heads, "dp", step) for step in range(1, replica_count)]

    terms = lax.all_to_all(terms, "tensor", 0, 0, tiled=True)
    embedded = jnp.sum(terms.astype(jnp.float32), axis=0).astype(jnp.bfloat16)
    spare = jnp.zeros((group_rows, -(head_rows * replica_count) % 128), jnp.bfloat16)
    parcel = lax.all_gather(
        jnp.concatenate([embedded, *past_all, spare], axis=1), "section", axis=0, tiled=True
    )
    visual_rows = parcel[:, :model_rows]
    past_rows = jnp.concatenate(
        [
            parcel[:, model_rows + step * head_rows : model_rows + (step + 1) * head_rows]
            for step in range(replica_count)
        ],
        axis=0,
    )
    placed = lax.dot_general(
        slot_table, visual_rows, (((0,), (0,)), ((), ())), preferred_element_type=jnp.float32
    ).astype(jnp.bfloat16)
    covered = jnp.sum(slot_table, axis=0, dtype=jnp.float32)
    inputs = jnp.where(first_flag & (covered[:, None] > 0.5), placed, layer_input[0].T)

    products, input_grad, visual_grad = section_products(
        pre_full, inputs, weight, layer_cotangent[0].T, past_slot
    )
    preact = lax.psum_scatter(products, "tensor", scatter_dimension=1, tiled=True).astype(
        jnp.float32
    )
    hidden = (inputs.astype(jnp.float32) + jax.nn.silu(preact)).astype(jnp.bfloat16)
    backward_out = shift(input_grad, "section", -1)

    base = to_relays(visual_grad)
    piece, backward_out = lax.optimization_barrier((spread_columns(base), backward_out))
    gathered = lax.all_gather(piece, "tensor", axis=0)
    per_block = tensor_count // BLOCK
    part_width = model_rows // replica_count
    position, replica = lax.rem(own_section + 1, BLOCK), lax.axis_index("dp")
    gathered = gathered.reshape(per_block, replica_count * visual_count, part_width)
    own_columns, head_part = [], 0.0
    for j in range(per_block):
        own_columns.append(
            lax.dot_general(
                past_rows, gathered[j], (((0,), (0,)), ((), ())), preferred_element_type=jnp.float32
            ).astype(jnp.bfloat16)
        )
        proj_part = lax.dynamic_slice_in_dim(
            visual_proj,
            (position * per_block + j) * model_rows + replica * part_width,
            part_width,
            axis=1,
        )
        proj_part = jnp.pad(proj_part, ((0, part_width - head_rows), (0, 0)))
        head_part = head_part + lax.dot_general(
            gathered[j], proj_part, (((1,), (1,)), ((), ())), preferred_element_type=jnp.float32
        )
    own_columns = jnp.concatenate(own_columns, axis=0)
    head_part = head_part.astype(jnp.bfloat16).reshape(
        replica_count, section_count, group_rows, part_width
    )

    def head_of(section):
        return lax.dynamic_index_in_dim(head_part, section, axis=1, keepdims=False).reshape(
            replica_count * group_rows, part_width
        )

    column_rows = own_columns.shape[0]
    in_block, head_sum = [own_columns], head_of(own_section).astype(jnp.float32)
    for step in range(1, BLOCK):
        hops = step if step <= BLOCK // 2 else step - BLOCK
        target = lax.rem(own_section + hops + section_count, section_count)
        arrived = rotate(
            jnp.concatenate([own_columns, head_of(target)], axis=0), "section", hops
        )
        in_block.append(arrived[:column_rows])
        head_sum = head_sum + arrived[column_rows:].astype(jnp.float32)

    bundle = jnp.concatenate(in_block + [head_sum.astype(jnp.bfloat16)], axis=0)
    arrived = [rotate(bundle, "dp", step) for step in range(1, replica_count)]
    forward_out = shift(hidden, "section", 1)
    *arrived, _ = lax.optimization_barrier((*arrived, hidden))
    head_grad = head_sum[:group_rows]
    for step in range(1, replica_count):
        first = BLOCK * column_rows + (replica_count - step) * group_rows
        head_grad = head_grad + arrived[step - 1][first : first + group_rows].astype(jnp.float32)
    head_grad = head_grad[:, :head_rows].astype(jnp.bfloat16)
    grad_proj = place_columns(
        jnp.stack([position, replica]).astype(jnp.int32),
        (bundle, *arrived),
        (per_block, head_rows, part_width),
    )
    frame_grads = attend_grad(past_saved, head_grad)
    return (forward_out.T[None], backward_out.T[None], grad_proj, frame_grads[:, None, None])


def solution(mesh):
    in_specs = (
        P("section", "dp", "tensor", None),
        P("section", "dp", "tensor", None),
        P("section", "dp", "tensor", None),
        P("section", "dp", None),
        P("section", "dp", "tensor", None),
        P("section", "dp", "tensor", None),
        P("section", "dp", "tensor", None),
        P("section", "dp", None),
        P("dp", None),
        P("dp", None),
        P("tensor", None),
        P("section", "tensor", None),
        P("section", "tensor", "dp"),
        P("section", "tensor", "dp"),
        P("section", "tensor", "dp"),
    )
    out_specs = (
        P("section", "tensor", "dp"),
        P("section", "tensor", "dp"),
        P("tensor", None),
        P(None, "section", "dp", "tensor", None),
    )
    return jax.shard_map(local, mesh=mesh, in_specs=in_specs, out_specs=out_specs, check_vma=False)
```

```python
import functools

import jax
import jax.numpy as jnp
from jax import lax
from jax.experimental import pallas as pl
from jax.experimental.pallas import tpu as pltpu
from jax.sharding import PartitionSpec as P

HEAD_DIM = 80


SCORE_FLOOR = -1e30


def attend_parts(query_rows, key_rows, value_rows, segment):
    scores = lax.dot_general(
        query_rows, key_rows, (((0,), (0,)), ((), ())), preferred_element_type=jnp.float32
    ) * HEAD_DIM ** (-0.5)
    same_sample = segment[:, None] == segment[None, :]
    scores = jnp.where(same_sample, scores, SCORE_FLOOR)
    row_peak = jnp.max(scores, axis=1, keepdims=True)
    exponent = jnp.exp(scores - row_peak)
    share = exponent / jnp.sum(exponent, axis=1, keepdims=True)
    weights = share.astype(jnp.bfloat16)
    mixed = lax.dot_general(
        weights, value_rows, (((1,), (1,)), ((), ())), preferred_element_type=jnp.float32
    )
    return mixed.astype(jnp.bfloat16), (query_rows, key_rows, value_rows, share, weights)


def attend_grad(saved, out_grad):
    query_rows, key_rows, value_rows, share, weights = saved
    weight_grad = jnp.dot(out_grad, value_rows, preferred_element_type=jnp.float32)
    score_grad = (
        share
        * (weight_grad - jnp.sum(weight_grad * share, axis=1, keepdims=True))
        * HEAD_DIM ** (-0.5)
    )
    query_grad = lax.dot_general(
        key_rows.astype(jnp.float32),
        score_grad,
        (((1,), (1,)), ((), ())),
        precision=lax.Precision.HIGHEST,
    )
    key_grad = jnp.dot(
        query_rows.astype(jnp.float32), score_grad, precision=lax.Precision.HIGHEST
    )
    value_grad = lax.dot_general(
        out_grad, weights, (((0,), (0,)), ((), ())), preferred_element_type=jnp.float32
    )
    return jnp.stack([query_grad, key_grad, value_grad])


def silu_slope(preact):
    sigmoid_value = jax.nn.sigmoid(preact)
    return sigmoid_value * (1.0 + preact * (1.0 - sigmoid_value))


def shift(value, axis, steps):
    count = lax.axis_size(axis)
    first, last = (max(0, -steps), min(count, count - steps))
    return lax.ppermute(value, axis, [(source, source + steps) for source in range(first, last)])


def rotate(value, axis, steps):
    count = lax.axis_size(axis)
    return lax.ppermute(value, axis, [(i, (i + steps) % count) for i in range(count)])


BLOCK = 4


def to_relays(value):
    count = lax.axis_size("section")
    own = lax.axis_index("section")
    base = jnp.where(own == 0, value, jnp.zeros_like(value))
    arrived = [lax.ppermute(value, "section", [(0, relay)]) for relay in range(BLOCK, count, BLOCK)]
    for piece in arrived:
        base = base + piece
    return base


def block_place(position, relay, count):
    return (relay + position - 1) % count


def spread_columns(base):
    sections, tensors, replicas = (lax.axis_size(axis) for axis in ("section", "tensor", "dp"))
    own = lax.axis_index("dp")
    width = base.shape[1] // replicas
    per_block = tensors // BLOCK

    def device(section, tensor, replica):
        return (section * tensors + tensor) * replicas + replica

    total = None
    for step in range(replicas):
        pairs = [
            (
                device(relay, per_block * position + j, replica),
                device(
                    block_place(position, relay, sections),
                    replicas * j + step,
                    (replica + step) % replicas,
                ),
            )
            for relay in range(0, sections, BLOCK)
            for position in range(BLOCK)
            for j in range(per_block)
            for replica in range(replicas)
        ]
        part = lax.dynamic_slice_in_dim(
            base, lax.rem(own + step, replicas) * width, width, axis=1
        )
        piece = lax.ppermute(part, ("section", "tensor", "dp"), pairs)
        total = piece if total is None else total + piece
    return total


def place_kernel(shape, own_ref, *refs):
    per_block, rows, width = shape
    pieces, out_ref = refs[:-1], refs[-1]
    position, replica = own_ref[0], own_ref[1]
    replicas = len(pieces)
    for step in range(replicas):
        source = lax.rem(replica - step + replicas, replicas)
        for back in range(BLOCK):
            place = lax.rem(position - back + BLOCK, BLOCK)
            for j in range(per_block):
                first = (back * per_block + j) * rows
                column = ((place * per_block + j) * replicas + source) * width
                out_ref[:, pl.ds(pl.multiple_of(column, width), width)] = pieces[step][
                    first : first + rows, :
                ]


def place_columns(own, pieces, shape):
    per_block, rows, width = shape
    return pl.pallas_call(
        functools.partial(place_kernel, shape),
        out_shape=jax.ShapeDtypeStruct(
            (rows, len(pieces) * BLOCK * per_block * width), jnp.bfloat16
        ),
        in_specs=[pl.BlockSpec(memory_space=pltpu.SMEM)]
        + [pl.BlockSpec(memory_space=pltpu.VMEM)] * len(pieces),
        out_specs=pl.BlockSpec(memory_space=pltpu.VMEM),
        compiler_params=pltpu.CompilerParams(vmem_limit_bytes=16 * 1024 * 1024),
    )(own, *pieces)


def section_kernel(
    flag_ref,
    cotangent_ref,
    parcel_ref,
    visual_slot_ref,
    text_ref,
    weight_ref,
    upstream_ref,
    past_slot_ref,
    product_ref,
    grad_ref,
    picked_ref,
    inputs_ref,
    total,
):
    step = pl.program_id(0)
    tokens, rows = text_ref.shape

    def table(slot_ref):
        positions = lax.broadcasted_iota(jnp.int32, (tokens, slot_ref.shape[1]), 0)
        return (positions == slot_ref[...]).astype(jnp.float32)

    @pl.when(step == 0)
    def _():
        total[...] = upstream_ref[...].astype(jnp.float32)
        slots = table(visual_slot_ref)
        placed = jnp.dot(
            slots.astype(jnp.bfloat16), parcel_ref[...], preferred_element_type=jnp.float32
        )
        covered = jnp.sum(slots, axis=1, keepdims=True) * flag_ref[0].astype(jnp.float32)
        inputs_ref[...] = jnp.where(
            jnp.broadcast_to(covered, (tokens, rows)) > 0.5,
            placed,
            text_ref[...].astype(jnp.float32),
        ).astype(jnp.bfloat16)

    total[...] += lax.dot_general(
        cotangent_ref[...],
        weight_ref[...],
        (((1,), (1,)), ((), ())),
        preferred_element_type=jnp.float32,
    )
    product_ref[...] = jnp.dot(
        inputs_ref[...], weight_ref[...], preferred_element_type=jnp.float32
    ).astype(jnp.bfloat16)

    @pl.when(step == pl.num_programs(0) - 1)
    def _():
        grad = total[...].astype(jnp.bfloat16)
        grad_ref[...] = grad
        picked_ref[...] = lax.dot_general(
            table(past_slot_ref).astype(jnp.bfloat16),
            grad,
            (((0,), (0,)), ((), ())),
            preferred_element_type=jnp.float32,
        ).astype(jnp.bfloat16)


def section_products(flag, cotangent, parcel, visual_slot, text, weight, upstream, past_slot):
    tokens, rows = text.shape
    width = weight.shape[1]
    tile = 2048
    whole = pl.BlockSpec((tokens, rows), lambda n: (0, 0))
    slots = pl.BlockSpec(past_slot.shape, lambda n: (0, 0))
    rows_shape = jax.ShapeDtypeStruct((tokens, rows), jnp.bfloat16)
    count = past_slot.shape[1]
    return pl.pallas_call(
        section_kernel,
        grid=(width // tile,),
        in_specs=[
            pl.BlockSpec(memory_space=pltpu.SMEM),
            pl.BlockSpec((tokens, tile), lambda n: (0, n)),
            pl.BlockSpec((parcel.shape[0], rows), lambda n: (0, 0)),
            slots,
            whole,
            pl.BlockSpec((rows, tile), lambda n: (0, n)),
            whole,
            slots,
        ],
        out_specs=[
            pl.BlockSpec((tokens, tile), lambda n: (0, n)),
            whole,
            pl.BlockSpec((count, rows), lambda n: (0, 0)),
            whole,
        ],
        out_shape=[
            jax.ShapeDtypeStruct((tokens, width), jnp.bfloat16),
            rows_shape,
            jax.ShapeDtypeStruct((count, rows), jnp.bfloat16),
            rows_shape,
        ],
        scratch_shapes=[pltpu.VMEM((tokens, rows), jnp.float32)],
        compiler_params=pltpu.CompilerParams(vmem_limit_bytes=56 * 1024 * 1024),
        cost_estimate=pl.CostEstimate(
            flops=4 * tokens * rows * width,
            bytes_accessed=2 * (rows * width + 2 * tokens * width),
            transcendentals=0,
        ),
    )(flag, cotangent, parcel, visual_slot, text, weight, upstream, past_slot)


def local(
    frame_query,
    frame_key,
    frame_value,
    frame_segment,
    past_query,
    past_key,
    past_value,
    past_segment,
    visual_slot,
    past_slot,
    visual_proj,
    layer_weight,
    layer_input,
    saved_preact,
    layer_cotangent,
):
    section_count = lax.axis_size("section")
    tensor_count = lax.axis_size("tensor")
    replica_count = lax.axis_size("dp")
    own_section = lax.axis_index("section")
    first_flag = own_section == 0
    model_rows = layer_weight.shape[1]
    head_rows = visual_proj.shape[0]
    group_rows = frame_query.shape[3]
    token_count = layer_input.shape[2]
    visual_count = section_count * group_rows
    weight = layer_weight[0]

    upstream = layer_cotangent[0].T.astype(jnp.float32)
    pre_grad = (upstream * silu_slope(saved_preact[0].T.astype(jnp.float32))).astype(jnp.bfloat16)
    pre_full = lax.all_gather(pre_grad, "tensor", axis=1, tiled=True)

    current, _ = attend_parts(
        frame_query[0, 0], frame_key[0, 0], frame_value[0, 0], frame_segment[0, 0]
    )
    terms = jnp.dot(current, visual_proj, preferred_element_type=jnp.float32).astype(jnp.bfloat16)
    terms = jnp.transpose(terms.reshape(group_rows, tensor_count, model_rows), (1, 0, 2))
    terms, past_query, past_key = lax.optimization_barrier((terms, past_query, past_key))
    past_heads, past_saved = attend_parts(
        past_query[0, 0], past_key[0, 0], past_value[0, 0], past_segment[0, 0]
    )

    past_all = [past_heads] + [rotate(past_heads, "dp", step) for step in range(1, replica_count)]

    terms = lax.all_to_all(terms, "tensor", 0, 0, tiled=True)
    embedded = jnp.sum(terms.astype(jnp.float32), axis=0).astype(jnp.bfloat16)
    spare = jnp.zeros((group_rows, -(head_rows * replica_count) % 128), jnp.bfloat16)
    parcel = lax.all_gather(
        jnp.concatenate([embedded, *past_all, spare], axis=1), "section", axis=0, tiled=True
    )
    past_rows = jnp.concatenate(
        [
            parcel[:, model_rows + step * head_rows : model_rows + (step + 1) * head_rows]
            for step in range(replica_count)
        ],
        axis=0,
    )
    products, input_grad, visual_grad, inputs = section_products(
        first_flag.astype(jnp.int32)[None],
        pre_full,
        parcel,
        visual_slot,
        layer_input[0].T,
        weight,
        layer_cotangent[0].T,
        past_slot,
    )
    preact = lax.psum_scatter(products, "tensor", scatter_dimension=1, tiled=True).astype(
        jnp.float32
    )
    hidden = (inputs.astype(jnp.float32) + jax.nn.silu(preact)).astype(jnp.bfloat16)
    backward_out = shift(input_grad, "section", -1)

    base = to_relays(visual_grad)
    piece, backward_out = lax.optimization_barrier((spread_columns(base), backward_out))
    gathered = lax.all_gather(piece, "tensor", axis=0)
    per_block = tensor_count // BLOCK
    part_width = model_rows // replica_count
    position, replica = lax.rem(own_section + 1, BLOCK), lax.axis_index("dp")
    gathered = gathered.reshape(per_block, replica_count * visual_count, part_width)
    own_columns, head_part = [], 0.0
    for j in range(per_block):
        own_columns.append(
            lax.dot_general(
                past_rows, gathered[j], (((0,), (0,)), ((), ())), preferred_element_type=jnp.float32
            ).astype(jnp.bfloat16)
        )
        proj_part = lax.dynamic_slice_in_dim(
            visual_proj,
            (position * per_block + j) * model_rows + replica * part_width,
            part_width,
            axis=1,
        )
        proj_part = jnp.pad(proj_part, ((0, part_width - head_rows), (0, 0)))
        head_part = head_part + lax.dot_general(
            gathered[j], proj_part, (((1,), (1,)), ((), ())), preferred_element_type=jnp.float32
        )
    own_columns = jnp.concatenate(own_columns, axis=0)
    head_part = head_part.astype(jnp.bfloat16).reshape(
        replica_count, section_count, group_rows, part_width
    )

    def head_of(section):
        return lax.dynamic_index_in_dim(head_part, section, axis=1, keepdims=False).reshape(
            replica_count * group_rows, part_width
        )

    column_rows, group_total = own_columns.shape[0], replica_count * group_rows

    def section_at(hops):
        return lax.rem(own_section + hops + section_count, section_count)

    before = rotate(
        jnp.concatenate([head_of(section_at(1)), own_columns, head_of(section_at(2))], axis=0),
        "section",
        1,
    )
    after = rotate(
        jnp.concatenate([head_of(section_at(-1)), own_columns], axis=0), "section", -1
    )
    second = rotate(before[group_total:], "section", 1)
    in_block = [
        own_columns,
        before[group_total : group_total + column_rows],
        second[:column_rows],
        after[group_total:],
    ]
    head_sum = head_of(own_section).astype(jnp.float32)
    for terms in (before[:group_total], second[column_rows:], after[:group_total]):
        head_sum = head_sum + terms.astype(jnp.float32)

    bundle = jnp.concatenate(in_block + [head_sum.astype(jnp.bfloat16)], axis=0)
    arrived = [rotate(bundle, "dp", step) for step in range(1, replica_count)]
    forward_out = shift(hidden, "section", 1)
    *arrived, _ = lax.optimization_barrier((*arrived, hidden))
    head_grad = head_sum[:group_rows]
    for step in range(1, replica_count):
        first = BLOCK * column_rows + (replica_count - step) * group_rows
        head_grad = head_grad + arrived[step - 1][first : first + group_rows].astype(jnp.float32)
    head_grad = head_grad[:, :head_rows].astype(jnp.bfloat16)
    grad_proj = place_columns(
        jnp.stack([position, replica]).astype(jnp.int32),
        (bundle, *arrived),
        (per_block, head_rows, part_width),
    )
    head_grad, forward_out = lax.optimization_barrier((head_grad, forward_out))
    frame_grads = attend_grad(past_saved, head_grad)
    return (forward_out.T[None], backward_out.T[None], grad_proj, frame_grads[:, None, None])


def solution(mesh):
    in_specs = (
        P("section", "dp", "tensor", None),
        P("section", "dp", "tensor", None),
        P("section", "dp", "tensor", None),
        P("section", "dp", None),
        P("section", "dp", "tensor", None),
        P("section", "dp", "tensor", None),
        P("section", "dp", "tensor", None),
        P("section", "dp", None),
        P("dp", None),
        P("dp", None),
        P("tensor", None),
        P("section", "tensor", None),
        P("section", "tensor", "dp"),
        P("section", "tensor", "dp"),
        P("section", "tensor", "dp"),
    )
    out_specs = (
        P("section", "tensor", "dp"),
        P("section", "tensor", "dp"),
        P("tensor", None),
        P(None, "section", "dp", "tensor", None),
    )
    return jax.shard_map(local, mesh=mesh, in_specs=in_specs, out_specs=out_specs, check_vma=False)
```

```python
import functools

import jax
import jax.numpy as jnp
from jax import lax
from jax.experimental import pallas as pl
from jax.experimental.pallas import tpu as pltpu
from jax.sharding import PartitionSpec as P

HEAD_DIM = 80


SCORE_FLOOR = -1e30


def attend_parts(query_rows, key_rows, value_rows, segment):
    scores = lax.dot_general(
        query_rows, key_rows, (((0,), (0,)), ((), ())), preferred_element_type=jnp.float32
    ) * HEAD_DIM ** (-0.5)
    same_sample = segment[:, None] == segment[None, :]
    scores = jnp.where(same_sample, scores, SCORE_FLOOR)
    row_peak = jnp.max(scores, axis=1, keepdims=True)
    exponent = jnp.exp(scores - row_peak)
    share = exponent / jnp.sum(exponent, axis=1, keepdims=True)
    weights = share.astype(jnp.bfloat16)
    mixed = lax.dot_general(
        weights, value_rows, (((1,), (1,)), ((), ())), preferred_element_type=jnp.float32
    )
    return mixed.astype(jnp.bfloat16), (query_rows, key_rows, value_rows, share, weights)


def attend_grad(saved, out_grad):
    query_rows, key_rows, value_rows, share, weights = saved
    weight_grad = jnp.dot(out_grad, value_rows, preferred_element_type=jnp.float32)
    score_grad = (
        share
        * (weight_grad - jnp.sum(weight_grad * share, axis=1, keepdims=True))
        * HEAD_DIM ** (-0.5)
    )
    query_grad = lax.dot_general(
        key_rows.astype(jnp.float32),
        score_grad,
        (((1,), (1,)), ((), ())),
        precision=lax.Precision.HIGHEST,
    )
    key_grad = jnp.dot(
        query_rows.astype(jnp.float32), score_grad, precision=lax.Precision.HIGHEST
    )
    value_grad = lax.dot_general(
        out_grad, weights, (((0,), (0,)), ((), ())), preferred_element_type=jnp.float32
    )
    return jnp.stack([query_grad, key_grad, value_grad])


def silu_slope(preact):
    sigmoid_value = jax.nn.sigmoid(preact)
    return sigmoid_value * (1.0 + preact * (1.0 - sigmoid_value))


def shift(value, axis, steps):
    count = lax.axis_size(axis)
    first, last = (max(0, -steps), min(count, count - steps))
    return lax.ppermute(value, axis, [(source, source + steps) for source in range(first, last)])


def rotate(value, axis, steps):
    count = lax.axis_size(axis)
    return lax.ppermute(value, axis, [(i, (i + steps) % count) for i in range(count)])


def rotate_apart(value, steps):
    tensors, count = lax.axis_size("tensor"), lax.axis_size("dp")
    pairs = [
        (t * count + r, t * count + (r + (steps if t % 2 == 0 else -steps)) % count)
        for t in range(tensors)
        for r in range(count)
    ]
    return lax.ppermute(value, ("tensor", "dp"), pairs)


BLOCK = 4


def to_relays(value):
    count = lax.axis_size("section")
    own = lax.axis_index("section")
    base = jnp.where(own == 0, value, jnp.zeros_like(value))
    arrived = [lax.ppermute(value, "section", [(0, relay)]) for relay in range(BLOCK, count, BLOCK)]
    for piece in arrived:
        base = base + piece
    return base


def block_place(position, relay, count):
    return (relay + position - 1) % count


def spread_columns(base):
    sections, tensors, replicas = (lax.axis_size(axis) for axis in ("section", "tensor", "dp"))
    own = lax.axis_index("dp")
    width = base.shape[1] // replicas
    per_block = tensors // BLOCK

    def device(section, tensor, replica):
        return (section * tensors + tensor) * replicas + replica

    total = None
    for step in range(replicas):
        pairs = [
            (
                device(relay, per_block * position + j, replica),
                device(
                    block_place(position, relay, sections),
                    replicas * j + step,
                    (replica + step) % replicas,
                ),
            )
            for relay in range(0, sections, BLOCK)
            for position in range(BLOCK)
            for j in range(per_block)
            for replica in range(replicas)
        ]
        part = lax.dynamic_slice_in_dim(
            base, lax.rem(own + step, replicas) * width, width, axis=1
        )
        piece = lax.ppermute(part, ("section", "tensor", "dp"), pairs)
        total = piece if total is None else total + piece
    return total


def place_kernel(shape, own_ref, *refs):
    per_block, rows, width = shape
    pieces, out_ref = refs[:-1], refs[-1]
    position, replica, odd = own_ref[0], own_ref[1], own_ref[2]
    replicas = len(pieces)
    for step, back_by in enumerate((0, 1 + 2 * odd, 2, 3 - 2 * odd)):
        source = lax.rem(replica - back_by + replicas, replicas)
        for back in range(BLOCK):
            place = lax.rem(position - back + BLOCK, BLOCK)
            for j in range(per_block):
                first = (back * per_block + j) * rows
                column = ((place * per_block + j) * replicas + source) * width
                out_ref[:, pl.ds(pl.multiple_of(column, width), width)] = pieces[step][
                    first : first + rows, :
                ]


def place_columns(own, pieces, shape):
    per_block, rows, width = shape
    return pl.pallas_call(
        functools.partial(place_kernel, shape),
        out_shape=jax.ShapeDtypeStruct(
            (rows, len(pieces) * BLOCK * per_block * width), jnp.bfloat16
        ),
        in_specs=[pl.BlockSpec(memory_space=pltpu.SMEM)]
        + [pl.BlockSpec(memory_space=pltpu.VMEM)] * len(pieces),
        out_specs=pl.BlockSpec(memory_space=pltpu.VMEM),
        compiler_params=pltpu.CompilerParams(vmem_limit_bytes=16 * 1024 * 1024),
    )(own, *pieces)


def section_kernel(
    flag_ref,
    cotangent_ref,
    parcel_ref,
    visual_slot_ref,
    text_ref,
    weight_ref,
    upstream_ref,
    past_slot_ref,
    product_ref,
    grad_ref,
    picked_ref,
    inputs_ref,
    total,
):
    step = pl.program_id(0)
    tokens, rows = text_ref.shape

    def table(slot_ref):
        positions = lax.broadcasted_iota(jnp.int32, (tokens, slot_ref.shape[1]), 0)
        return (positions == slot_ref[...]).astype(jnp.float32)

    @pl.when(step == 0)
    def _():
        total[...] = upstream_ref[...].astype(jnp.float32)
        slots = table(visual_slot_ref)
        placed = jnp.dot(
            slots.astype(jnp.bfloat16), parcel_ref[...], preferred_element_type=jnp.float32
        )
        covered = jnp.sum(slots, axis=1, keepdims=True) * flag_ref[0].astype(jnp.float32)
        inputs_ref[...] = jnp.where(
            jnp.broadcast_to(covered, (tokens, rows)) > 0.5,
            placed,
            text_ref[...].astype(jnp.float32),
        ).astype(jnp.bfloat16)

    total[...] += lax.dot_general(
        cotangent_ref[...],
        weight_ref[...],
        (((1,), (1,)), ((), ())),
        preferred_element_type=jnp.float32,
    )
    product_ref[...] = jnp.dot(
        inputs_ref[...], weight_ref[...], preferred_element_type=jnp.float32
    ).astype(jnp.bfloat16)

    @pl.when(step == pl.num_programs(0) - 1)
    def _():
        grad = total[...].astype(jnp.bfloat16)
        grad_ref[...] = grad
        picked_ref[...] = lax.dot_general(
            table(past_slot_ref).astype(jnp.bfloat16),
            grad,
            (((0,), (0,)), ((), ())),
            preferred_element_type=jnp.float32,
        ).astype(jnp.bfloat16)


def section_products(flag, cotangent, parcel, visual_slot, text, weight, upstream, past_slot):
    tokens, rows = text.shape
    width = weight.shape[1]
    tile = 4096
    whole = pl.BlockSpec((tokens, rows), lambda n: (0, 0))
    slots = pl.BlockSpec(past_slot.shape, lambda n: (0, 0))
    rows_shape = jax.ShapeDtypeStruct((tokens, rows), jnp.bfloat16)
    count = past_slot.shape[1]
    return pl.pallas_call(
        section_kernel,
        grid=(width // tile,),
        in_specs=[
            pl.BlockSpec(memory_space=pltpu.SMEM),
            pl.BlockSpec((tokens, tile), lambda n: (0, n)),
            pl.BlockSpec((parcel.shape[0], rows), lambda n: (0, 0)),
            slots,
            whole,
            pl.BlockSpec((rows, tile), lambda n: (0, n)),
            whole,
            slots,
        ],
        out_specs=[
            pl.BlockSpec((tokens, tile), lambda n: (0, n)),
            whole,
            pl.BlockSpec((count, rows), lambda n: (0, 0)),
            whole,
        ],
        out_shape=[
            jax.ShapeDtypeStruct((tokens, width), jnp.bfloat16),
            rows_shape,
            jax.ShapeDtypeStruct((count, rows), jnp.bfloat16),
            rows_shape,
        ],
        scratch_shapes=[pltpu.VMEM((tokens, rows), jnp.float32)],
        compiler_params=pltpu.CompilerParams(vmem_limit_bytes=56 * 1024 * 1024),
        cost_estimate=pl.CostEstimate(
            flops=4 * tokens * rows * width,
            bytes_accessed=2 * (rows * width + 2 * tokens * width),
            transcendentals=0,
        ),
    )(flag, cotangent, parcel, visual_slot, text, weight, upstream, past_slot)


def local(
    frame_query,
    frame_key,
    frame_value,
    frame_segment,
    past_query,
    past_key,
    past_value,
    past_segment,
    visual_slot,
    past_slot,
    visual_proj,
    layer_weight,
    layer_input,
    saved_preact,
    layer_cotangent,
):
    section_count = lax.axis_size("section")
    tensor_count = lax.axis_size("tensor")
    replica_count = lax.axis_size("dp")
    own_section = lax.axis_index("section")
    first_flag = own_section == 0
    model_rows = layer_weight.shape[1]
    head_rows = visual_proj.shape[0]
    group_rows = frame_query.shape[3]
    token_count = layer_input.shape[2]
    visual_count = section_count * group_rows
    weight = layer_weight[0]

    upstream = layer_cotangent[0].T.astype(jnp.float32)
    pre_grad = (upstream * silu_slope(saved_preact[0].T.astype(jnp.float32))).astype(jnp.bfloat16)
    pre_full = lax.all_gather(pre_grad, "tensor", axis=1, tiled=True)

    current, _ = attend_parts(
        frame_query[0, 0], frame_key[0, 0], frame_value[0, 0], frame_segment[0, 0]
    )
    terms = jnp.dot(current, visual_proj, preferred_element_type=jnp.float32).astype(jnp.bfloat16)
    terms = jnp.transpose(terms.reshape(group_rows, tensor_count, model_rows), (1, 0, 2))
    terms, past_query, past_key = lax.optimization_barrier((terms, past_query, past_key))
    past_heads, past_saved = attend_parts(
        past_query[0, 0], past_key[0, 0], past_value[0, 0], past_segment[0, 0]
    )

    past_all = [past_heads] + [rotate(past_heads, "dp", step) for step in range(1, replica_count)]

    terms = lax.all_to_all(terms, "tensor", 0, 0, tiled=True)
    embedded = jnp.sum(terms.astype(jnp.float32), axis=0).astype(jnp.bfloat16)
    spare = jnp.zeros((group_rows, -(head_rows * replica_count) % 128), jnp.bfloat16)
    parcel = lax.all_gather(
        jnp.concatenate([embedded, *past_all, spare], axis=1), "section", axis=0, tiled=True
    )
    past_rows = jnp.concatenate(
        [
            parcel[:, model_rows + step * head_rows : model_rows + (step + 1) * head_rows]
            for step in range(replica_count)
        ],
        axis=0,
    )
    products, input_grad, visual_grad, inputs = section_products(
        first_flag.astype(jnp.int32)[None],
        pre_full,
        parcel,
        visual_slot,
        layer_input[0].T,
        weight,
        layer_cotangent[0].T,
        past_slot,
    )
    preact = lax.psum_scatter(products, "tensor", scatter_dimension=1, tiled=True).astype(
        jnp.float32
    )
    hidden = (inputs.astype(jnp.float32) + jax.nn.silu(preact)).astype(jnp.bfloat16)
    backward_out = shift(input_grad, "section", -1)

    base = to_relays(visual_grad)
    piece, backward_out = lax.optimization_barrier((spread_columns(base), backward_out))
    gathered = lax.all_gather(piece, "tensor", axis=0)
    per_block = tensor_count // BLOCK
    part_width = model_rows // replica_count
    position, replica = lax.rem(own_section + 1, BLOCK), lax.axis_index("dp")
    gathered = gathered.reshape(per_block, replica_count * visual_count, part_width)
    own_columns, head_part = [], 0.0
    for j in range(per_block):
        own_columns.append(
            lax.dot_general(
                past_rows, gathered[j], (((0,), (0,)), ((), ())), preferred_element_type=jnp.float32
            ).astype(jnp.bfloat16)
        )
        proj_part = lax.dynamic_slice_in_dim(
            visual_proj,
            (position * per_block + j) * model_rows + replica * part_width,
            part_width,
            axis=1,
        )
        proj_part = jnp.pad(proj_part, ((0, part_width - head_rows), (0, 0)))
        head_part = head_part + lax.dot_general(
            gathered[j], proj_part, (((1,), (1,)), ((), ())), preferred_element_type=jnp.float32
        )
    own_columns = jnp.concatenate(own_columns, axis=0)
    head_part = head_part.astype(jnp.bfloat16).reshape(
        replica_count, section_count, group_rows, part_width
    )

    def head_of(section):
        return lax.dynamic_index_in_dim(head_part, section, axis=1, keepdims=False).reshape(
            replica_count * group_rows, part_width
        )

    column_rows, group_total = own_columns.shape[0], replica_count * group_rows

    def section_at(hops):
        return lax.rem(own_section + hops + section_count, section_count)

    before = rotate(
        jnp.concatenate([head_of(section_at(1)), own_columns, head_of(section_at(2))], axis=0),
        "section",
        1,
    )
    after = rotate(
        jnp.concatenate([head_of(section_at(-1)), own_columns], axis=0), "section", -1
    )
    second = rotate(before[group_total:], "section", 1)
    in_block = [
        own_columns,
        before[group_total : group_total + column_rows],
        second[:column_rows],
        after[group_total:],
    ]
    head_sum = head_of(own_section).astype(jnp.float32)
    for terms in (before[:group_total], second[column_rows:], after[:group_total]):
        head_sum = head_sum + terms.astype(jnp.float32)

    bundle = jnp.concatenate(in_block + [head_sum.astype(jnp.bfloat16)], axis=0)
    odd = lax.rem(lax.axis_index("tensor"), 2)
    arrived = [rotate_apart(bundle, 1), rotate(bundle, "dp", 2), rotate_apart(bundle, -1)]
    steps = [1 + 2 * odd, 2, 3 - 2 * odd]
    forward_out = shift(hidden, "section", 1)
    *arrived, _ = lax.optimization_barrier((*arrived, hidden))
    head_grad = head_sum[:group_rows]
    for step, bundle_there in zip(steps, arrived):
        first = BLOCK * column_rows + (replica_count - step) * group_rows
        head_grad = head_grad + lax.dynamic_slice_in_dim(
            bundle_there, first, group_rows, axis=0
        ).astype(jnp.float32)
    head_grad = head_grad[:, :head_rows].astype(jnp.bfloat16)
    grad_proj = place_columns(
        jnp.stack([position, replica, odd]).astype(jnp.int32),
        (bundle, *arrived),
        (per_block, head_rows, part_width),
    )
    head_grad, forward_out = lax.optimization_barrier((head_grad, forward_out))
    frame_grads = attend_grad(past_saved, head_grad)
    return (forward_out.T[None], backward_out.T[None], grad_proj, frame_grads[:, None, None])


def solution(mesh):
    in_specs = (
        P("section", "dp", "tensor", None),
        P("section", "dp", "tensor", None),
        P("section", "dp", "tensor", None),
        P("section", "dp", None),
        P("section", "dp", "tensor", None),
        P("section", "dp", "tensor", None),
        P("section", "dp", "tensor", None),
        P("section", "dp", None),
        P("dp", None),
        P("dp", None),
        P("tensor", None),
        P("section", "tensor", None),
        P("section", "tensor", "dp"),
        P("section", "tensor", "dp"),
        P("section", "tensor", "dp"),
    )
    out_specs = (
        P("section", "tensor", "dp"),
        P("section", "tensor", "dp"),
        P("tensor", None),
        P(None, "section", "dp", "tensor", None),
    )
    return jax.shard_map(local, mesh=mesh, in_specs=in_specs, out_specs=out_specs, check_vma=False)
```
